32 devices in a mesh: row: 4 (over y, x), col: 8 (over z, core).
Axes of the slice: x: 2, y: 2, z: 4, core: 2. Of those that a mesh axis runs over, the one named last changes fastest.
Arguments:
- tokens: bfloat16 [64, 12288], P('col', 'row'), may hold values from -6 to 6
- cotangent: bfloat16 [64, 12288], P('col', 'row'), may hold values from -6 to 6
- w1_mask: int32 [96, 384], P('row', 'col'), may hold values from 0 to 1, as said below
- w1_blocks: bfloat16 [4, 8, 288, 128, 128], P('row', 'col'), may hold values from -0.109375 to 0.109375
- bias: bfloat16 [49152], P('col'), may hold values from -4 to 4
- w2_mask: int32 [384, 96], P('col', 'row'), may hold values from 0 to 1, as said below
- w2_blocks: bfloat16 [4, 8, 288, 128, 128], P('row', 'col'), may hold values from -0.0546875 to 0.0546875
Outputs:
- out: bfloat16 [64, 12288], P('col', 'row')
- tokens_grad: bfloat16 [64, 12288], P('col', 'row')
- w1_grad: float32 [4, 8, 288, 128, 128], P('row', 'col')
- w2_grad: float32 [4, 8, 288, 128, 128], P('row', 'col')
- bias_grad: float32 [49152], P('col')
The draws below stay inside these ranges and needn't reach their ends.
Inputs may be any that keep to these rules, and one draw needn't show every extreme that they name: `w1_mask`: in every block row, each aligned group of 8 blocks along the columns holds exactly two ones. One device's tile of 24 x 48 blocks holds at most 288 ones, and in every draw some device's tile holds exactly 288. `w2_mask`: in every block row, each aligned group of 8 blocks along the columns holds exactly two ones. One device's tile of 48 x 24 blocks holds at most 288 ones, and in every draw some device's tile holds exactly 288.
All inputs are finite; a program needn't handle non-finite values.
Results may differ from the reference program's by a relative error of at most 0.005.
Values may be sent and summed in bfloat16 or wider, within the bound.
No kernel may reach another device: no remote copies, remote signals or barrier semaphores. Data moves between devices by JAX's collectives and lax.ppermute only.
A program may use at most 128 MiB of HBM per device.

```python
import math
import jax
import jax.numpy as jnp
from jax import lax

D = 12288
FF = 49152
BLK = 128
TOKENS = 64
TBR = 24
TBC = 48
CAP1 = 288
CAP2 = 288
N_ROW = 4
N_COL = 8


def pair_mask(key, row_count, col_count, tile_width, band_height):
    groups = col_count // 8
    splits = jax.random.split(key, 6)
    first_pos = jax.random.randint(splits[0], (row_count, groups), 0, 8)
    second_pos = (first_pos + jax.random.randint(splits[1], (row_count, groups), 1, 8)) % 8
    band_index = jax.random.randint(splits[2], (), 0, row_count // band_height)
    tile_index = jax.random.randint(splits[3], (), 0, col_count // tile_width)
    group_start = jnp.arange(groups) * 8
    low_edge = jnp.clip(tile_index * tile_width - group_start, 0, 8)
    high_edge = jnp.clip(tile_index * tile_width + tile_width - group_start, 0, 8)
    span_size = high_edge - low_edge
    offset_one = jax.random.randint(splits[4], (row_count, groups), 0, 1 << 20)
    offset_two = jax.random.randint(splits[5], (row_count, groups), 0, 1 << 20)
    safe_span = jnp.maximum(span_size, 2)[None, :]
    pick_one = offset_one % safe_span
    pick_two = (pick_one + 1 + offset_two % (safe_span - 1)) % safe_span
    inside = (jnp.arange(row_count)[:, None] // band_height == band_index) & (span_size[None, :] >= 2)
    first_pos = jnp.where(inside, low_edge[None, :] + pick_one, first_pos)
    second_pos = jnp.where(inside, low_edge[None, :] + pick_two, second_pos)
    places = jnp.arange(8)
    marks = (places == first_pos[..., None]) | (places == second_pos[..., None])
    return marks.reshape(row_count, col_count).astype(jnp.int32)


def draw_w1_mask(key, part):
    return pair_mask(jax.random.fold_in(key, 11), D // BLK, FF // BLK, TBC, TBR)


def draw_w2_mask(key, part):
    return pair_mask(jax.random.fold_in(key, 23), FF // BLK, D // BLK, TBR, TBC)


def block_levels(own_key, shape, cuts, least, top_value):
    gain, own = 1.0, jax.random.fold_in(own_key, 6)
    for dim, parts in cuts:
        steps = jnp.exp(jax.random.uniform(jax.random.fold_in(own, dim), (parts,), jnp.float32, least / len(cuts), top_value / len(cuts)))
        gain = gain * jnp.repeat(steps, shape[dim] // parts).reshape([-1 if axis == dim else 1 for axis in range(len(shape))])
    return gain


def centred(own_key, shape, deviation, reach, shards=(), held_as=jnp.bfloat16):
    result = jax.random.normal(own_key, shape, jnp.float32) * deviation
    if len(shards) > 0:
        result = block_levels(own_key, shape, shards, -0.22, 0.18) * result
    return jnp.clip(result, min=-reach, max=reach).astype(held_as)


def setup_inputs(seed: int = 0) -> dict:
    key_of = jax.random.split(jax.random.key(seed), 8)
    return {
        "tokens": centred(key_of[0], (TOKENS, D), 1.0, 6.0, ((0, 8), (1, 4))),
        "cotangent": centred(key_of[1], (TOKENS, D), 1.0, 6.0, ((0, 8), (1, 4))),
        "w1_mask": draw_w1_mask(jax.random.fold_in(key_of[7], 71), 0),
        "w1_blocks": centred(key_of[3], (N_ROW, N_COL, CAP1, BLK, BLK), (D // 4) ** -0.5, 0.109375, ((0, 4), (1, 8))),
        "bias": centred(key_of[4], (FF,), 1.0, 4.0, ((0, 8),)),
        "w2_mask": draw_w2_mask(jax.random.fold_in(key_of[7], 71), 0),
        "w2_blocks": centred(key_of[6], (N_ROW, N_COL, CAP2, BLK, BLK), (FF // 4) ** -0.5, 0.0546875, ((0, 4), (1, 8))),
    }


slope_const = math.sqrt(2.0 / math.pi)

def gelu_value(values):
    inner = slope_const * (values + 0.044715 * values * values * values)
    return 0.5 * values * (1.0 + jnp.tanh(inner))

def gelu_slope(values):
    inner = slope_const * (values + 0.044715 * values * values * values)
    tangent = jnp.tanh(inner)
    return 0.5 * (1.0 + tangent) + 0.5 * values * (1.0 - tangent * tangent) * slope_const * (1.0 + 3.0 * 0.044715 * values * values)

def slot_order(mask_tile, capacity):
    flat = mask_tile.reshape(-1)
    order = jnp.argsort(1 - flat, stable=True)[:capacity].astype(jnp.int32)
    live_slot = jnp.arange(capacity, dtype=jnp.int32) < jnp.sum(flat).astype(jnp.int32)
    return (order, live_slot)

def tile_dense(mask_tile, blocks):
    row_count, col_count = mask_tile.shape
    capacity = blocks.shape[0]
    block_width = blocks.shape[1]
    order, live_slot = slot_order(mask_tile, capacity)
    target = jnp.where(live_slot, order, row_count * col_count).astype(jnp.int32)
    dense = jnp.zeros((row_count * col_count + 1, block_width, block_width), blocks.dtype).at[target].set(blocks)
    dense = dense[:row_count * col_count]
    dense = dense.reshape(row_count, col_count, block_width, block_width).transpose(0, 2, 1, 3)
    return dense.reshape(row_count * block_width, col_count * block_width)

def tile_blocks(dense, mask_tile, capacity):
    row_count, col_count = mask_tile.shape
    block_width = dense.shape[0] // row_count
    pieces = dense.reshape(row_count, block_width, col_count, block_width).transpose(0, 2, 1, 3)
    pieces = pieces.reshape(row_count * col_count, block_width, block_width)
    order, live_slot = slot_order(mask_tile, capacity)
    return pieces[order] * live_slot[:, None, None].astype(jnp.float32)

def reference(tokens, cotangent, w1_mask, w1_blocks, bias, w2_mask, w2_blocks):
    hidden_width = TBC * BLK
    first_grid = w1_mask.reshape(N_ROW, TBR, N_COL, TBC)
    second_grid = w2_mask.reshape(N_COL, TBC, N_ROW, TBR)

    def column_step(running, column):
        out_acc, grad_acc = running
        first_masks = jnp.take(first_grid, column, axis=2)
        first_tiles = jnp.take(w1_blocks, column, axis=1)
        w1_column = jax.vmap(tile_dense)(first_masks, first_tiles).reshape(D, hidden_width)
        second_masks = jnp.take(second_grid, column, axis=0).transpose(1, 0, 2)
        second_tiles = jnp.take(w2_blocks, column, axis=1)
        w2_row = jax.vmap(tile_dense)(second_masks, second_tiles).transpose(1, 0, 2).reshape(hidden_width, D)
        bias_part = lax.dynamic_slice_in_dim(bias, column * hidden_width, hidden_width).astype(jnp.float32)
        hidden = jnp.dot(tokens, w1_column, preferred_element_type=jnp.float32) + bias_part
        activated = gelu_value(hidden).astype(jnp.bfloat16)
        out_acc = out_acc + jnp.dot(activated, w2_row, preferred_element_type=jnp.float32)
        grad_act = jnp.dot(cotangent, w2_row.T, preferred_element_type=jnp.float32)
        grad_hidden = (grad_act * gelu_slope(hidden)).astype(jnp.bfloat16)
        grad_acc = grad_acc + jnp.dot(grad_hidden, w1_column.T, preferred_element_type=jnp.float32)
        first_dense = jnp.dot(tokens.T, grad_hidden, preferred_element_type=jnp.float32).reshape(N_ROW, TBR * BLK, hidden_width)
        first_grad = jax.vmap(lambda dense, mask_tile: tile_blocks(dense, mask_tile, CAP1))(first_dense, first_masks)
        second_dense = jnp.dot(activated.T, cotangent, preferred_element_type=jnp.float32)
        second_dense = second_dense.reshape(hidden_width, N_ROW, TBR * BLK).transpose(1, 0, 2)
        second_grad = jax.vmap(lambda dense, mask_tile: tile_blocks(dense, mask_tile, CAP2))(second_dense, second_masks)
        bias_sum = lax.optimization_barrier(jnp.sum(grad_hidden.astype(jnp.float32), axis=0))
        return ((out_acc, grad_acc), (first_grad, second_grad, bias_sum))
    start = (jnp.zeros((TOKENS, D), jnp.float32), jnp.zeros((TOKENS, D), jnp.float32))
    (out_acc, grad_acc), (first_all, second_all, bias_all) = lax.scan(column_step, start, jnp.arange(N_COL, dtype=jnp.int32))
    w1_grad = first_all.transpose(1, 0, 2, 3, 4)
    w2_grad = second_all.transpose(1, 0, 2, 3, 4)
    return (out_acc.astype(jnp.bfloat16), grad_acc.astype(jnp.bfloat16), w1_grad, w2_grad, bias_all.reshape(-1))
```

```python
import math

import jax
import jax.numpy as jnp
from jax import lax
from jax.experimental import pallas as pl
from jax.experimental.pallas import tpu as pltpu
from jax.sharding import PartitionSpec as P

BLK = 128
F32 = jnp.float32
BF16 = jnp.bfloat16
VMEM_LIMIT = 40 * 1024 * 1024

slope_const = math.sqrt(2.0 / math.pi)


def gelu_parts(values):
    inner = slope_const * (values + 0.044715 * values * values * values)
    tangent = jnp.tanh(inner)
    value = 0.5 * values * (1.0 + tangent)
    slope = 0.5 * (1.0 + tangent) + 0.5 * values * (1.0 - tangent * tangent) * slope_const * (
        1.0 + 3.0 * 0.044715 * values * values
    )
    return value, slope


def swap(array, axis, size, mask):
    return lax.ppermute(array, axis, [(place, place ^ mask) for place in range(size)])


def call(body, outs, in_specs, args, scratch=(), grid=None, out_specs=None, flops=0, moved=0):
    whole = pl.BlockSpec(memory_space=pltpu.VMEM)
    extra = {} if grid is None else {"grid": grid}
    return pl.pallas_call(
        body,
        out_shape=outs,
        in_specs=in_specs,
        out_specs=[whole] * len(outs) if out_specs is None else out_specs,
        scratch_shapes=list(scratch),
        compiler_params=pltpu.CompilerParams(vmem_limit_bytes=VMEM_LIMIT),
        cost_estimate=pl.CostEstimate(flops=flops, bytes_accessed=moved, transcendentals=0),
        **extra,
    )(*args)


VM = pl.BlockSpec(memory_space=pltpu.VMEM)
SM = pl.BlockSpec(memory_space=pltpu.SMEM)


def shape_of(shape, dtype):
    return jax.ShapeDtypeStruct(shape, dtype)


def dot(left, right, left_dim, right_dim):
    return lax.dot_general(
        left, right, (((left_dim,), (right_dim,)), ((), ())), preferred_element_type=F32
    )


class Slots:
    def __init__(self, mask_shape, capacity):
        self.rows, self.cols = mask_shape
        self.capacity = capacity
        self.even = self.cols % 8 == 0 and capacity == self.rows * (self.cols // 4)
        self.group = self.cols // 4 if self.even else 1
        self.groups = capacity // self.group
        self.spare = 0 if self.even else 1

    def index_args(self, mask):
        flat = mask.reshape(-1)
        count = flat.shape[0]
        places = jnp.arange(count, dtype=jnp.int32)
        lane = jnp.arange(self.cols, dtype=jnp.int32)
        within = jnp.sum(jnp.where(lane[None, :] <= lane[:, None], mask[:, None, :], 0), axis=2)
        row_sum = jnp.sum(mask, axis=1)
        line = jnp.arange(self.rows, dtype=jnp.int32)
        before = jnp.sum(jnp.where(line[None, :] < line[:, None], row_sum[None, :], 0), axis=1)
        rank = (within + before[:, None] - 1).reshape(-1)
        slot = jnp.arange(self.capacity, dtype=jnp.int32)
        hit = (rank[None, :] == slot[:, None]) & (flat[None, :] > 0)
        order = jnp.sum(jnp.where(hit, places[None, :], 0), axis=1)
        live = slot < jnp.sum(flat)
        row = jnp.where(live, order // self.cols, self.rows)
        col = jnp.where(live, order % self.cols, self.cols)
        return row, col


def index_kernel(layouts, *refs):
    count = len(layouts)
    for layout, mask_ref, out_ref in zip(layouts, refs[:count], refs[count:]):
        rows, cols, group = layout.rows, layout.cols, layout.group
        mask = mask_ref[...].astype(F32)
        lower = lax.broadcasted_iota(jnp.int32, (cols, cols), 0)
        upper = lax.broadcasted_iota(jnp.int32, (cols, cols), 1)
        ramp = jnp.where(lower <= upper, 1.0, 0.0).astype(BF16)
        rank = dot(mask.astype(BF16), ramp, 1, 0)
        place = lax.broadcasted_iota(jnp.int32, (rows, cols), 1).astype(F32)
        lane = lax.broadcasted_iota(jnp.int32, (rows, BLK), 1)
        found = jnp.zeros((rows, BLK), F32)
        for slot in range(group):
            hit = (rank == float(slot + 1)) & (mask > 0.0)
            column = jnp.sum(jnp.where(hit, place, 0.0), axis=1, keepdims=True)
            found = jnp.where(lane == slot, column, found)
        out_ref[...] = found.astype(jnp.int32)


def slot_indices(layouts, masks):
    if all(layout.even and layout.group <= BLK for layout in layouts):
        outs = call(
            lambda *refs: index_kernel(layouts, *refs),
            [shape_of((layout.rows, BLK), jnp.int32) for layout in layouts],
            [VM] * len(layouts),
            masks,
        )
        return [(out, out) for out in outs]
    return [layout.index_args(mask) for layout, mask in zip(layouts, masks)]


def read_slot(layout, row_ref, col_ref, group, member):
    if layout.even:
        return group, col_ref[group, member]
    return row_ref[group], col_ref[group]


def add_forward(layout, row_ref, col_ref, first, here, source, blocks, total):
    group = layout.group
    for near in range(here):
        if layout.even:
            left = source[first + near]
            width = 2 if group % 2 == 0 else 1
            for member in range(0, group, width):
                place = near * group + member
                right = [blocks[place + more] for more in range(width)]
                right = right[0] if width == 1 else jnp.concatenate(right, axis=1)
                product = dot(left, right, 1, 0)
                for more in range(width):
                    col = col_ref[first + near, member + more]
                    total[col] += product[:, more * BLK : (more + 1) * BLK]
        else:
            row, col = read_slot(layout, row_ref, col_ref, first + near, 0)
            total[col] += dot(source[row], blocks[near], 1, 0)


def add_backward(layout, row_ref, col_ref, first, here, source, blocks, total):
    group = layout.group
    for near in range(here):
        if layout.even:
            width = 2 if group % 2 == 0 else 1
            result = None
            for member in range(0, group, width):
                place = near * group + member
                cols = [col_ref[first + near, member + more] for more in range(width)]
                left = [source[col] for col in cols]
                right = [blocks[place + more] for more in range(width)]
                left = left[0] if width == 1 else jnp.concatenate(left, axis=1)
                right = right[0] if width == 1 else jnp.concatenate(right, axis=1)
                product = dot(left, right, 1, 1)
                result = product if result is None else result + product
            total[first + near] = result
        else:
            row, col = read_slot(layout, row_ref, col_ref, first + near, 0)
            total[row] += dot(source[col], blocks[near], 1, 1)


def block_products(layout, row_ref, col_ref, first, here, left, right, out):
    group = layout.group
    for near in range(here):
        if layout.even:
            turned = left[first + near].T
            width = 2 if group % 2 == 0 else 1
            for member in range(0, group, width):
                place = near * group + member
                cols = [col_ref[first + near, member + more] for more in range(width)]
                wide = [right[col] for col in cols]
                wide = wide[0] if width == 1 else jnp.concatenate(wide, axis=1)
                product = dot(turned, wide, 1, 0)
                for more in range(width):
                    out[place + more] = product[:, more * BLK : (more + 1) * BLK]
        else:
            row, col = read_slot(layout, row_ref, col_ref, first + near, 0)
            live = row < layout.rows
            product = dot(left[row].T, right[col], 1, 0)
            out[near] = jnp.where(live, product, 0.0)


def gather_model(me, shards, stage, full):
    piece = shards[0].shape[0]
    for mask, shard in enumerate(shards):
        start = pl.multiple_of((me ^ mask) * piece, piece)
        stage[pl.ds(start, piece), :] = shard[...].astype(F32)
    for block in range(shards[0].shape[1] // BLK):
        full[block] = stage[:, block * BLK : (block + 1) * BLK].astype(full.dtype)


def gather_hidden(me, shares, full):
    blocks, piece, _ = shares[0].shape
    for mask, share in enumerate(shares):
        start = pl.multiple_of((me ^ mask) * piece, piece)
        full[pl.ds(0, blocks), pl.ds(start, piece), :] = share[...]


def steps_for(layout):
    for steps in (6, 4, 3, 2):
        if layout.groups % steps == 0:
            return steps
    return 1


def weight_spec(layout, steps):
    slots = layout.capacity // steps
    return pl.BlockSpec((slots, BLK, BLK), lambda step: (step, 0, 0))


def whole_spec(shape):
    rank = len(shape)
    return pl.BlockSpec(shape, lambda step: (0,) * rank)


def apply_cost(layout, tokens):
    return 2 * layout.capacity * BLK * BLK * tokens, 2 * layout.capacity * BLK * BLK


def model_to_hidden(layout, rows_cols, shards, blocks, forward, hidden_blocks, n_row):
    steps = steps_for(layout)
    here = layout.groups // steps
    count = len(shards)
    tokens = shards[0].shape[0] * count
    model_blocks = shards[0].shape[1] // BLK
    piece = tokens // n_row
    spare = layout.spare

    def body(row_ref, col_ref, *refs):
        parts = refs[:count]
        weights = refs[count]
        own, *sends, whole = refs[count + 1 : count + 2 + n_row]
        stage, full, total = refs[count + 2 + n_row :]
        step = pl.program_id(0)

        @pl.when(step == 0)
        def _():
            gather_model(lax.axis_index("col"), parts, stage, full)
            if spare:
                full[model_blocks] = jnp.zeros((tokens, BLK), BF16)
            total[...] = jnp.zeros_like(total)

        work = add_forward if forward else add_backward
        work(layout, row_ref, col_ref, step * here, here, full, weights, total)

        @pl.when(step == steps - 1)
        def _():
            me = lax.axis_index("row")
            whole[...] = full[pl.ds(0, model_blocks)]
            for mask, out in enumerate([own] + sends):
                start = pl.multiple_of((me ^ mask) * piece, piece)
                out[...] = total[pl.ds(0, hidden_blocks), pl.ds(start, piece), :].astype(out.dtype)

    share = (hidden_blocks, piece, BLK)
    outs = [shape_of(share, F32)] + [shape_of(share, BF16)] * (n_row - 1)
    outs += [shape_of((model_blocks, tokens, BLK), BF16)]
    flops, moved = apply_cost(layout, tokens)
    own, *rest = call(
        body,
        outs,
        [SM, SM] + [whole_spec(shards[0].shape)] * count + [weight_spec(layout, steps)],
        [*rows_cols, *shards, blocks],
        scratch=[
            pltpu.VMEM((tokens, model_blocks * BLK), F32),
            pltpu.VMEM((model_blocks + spare, tokens, BLK), BF16),
            pltpu.VMEM((hidden_blocks + spare, tokens, BLK), F32),
        ],
        grid=(steps,),
        out_specs=[whole_spec(out.shape) for out in outs],
        flops=flops,
        moved=moved,
    )
    return own, rest[:-1], rest[-1]


def hidden_to_model(layout, rows_cols, shares, blocks, forward, model_blocks, n_col, other=None):
    steps = steps_for(layout)
    here = layout.groups // steps
    count = len(shares)
    hidden_blocks, part, _ = shares[0].shape
    tokens = part * count
    piece = tokens // n_col
    half = n_col // 2
    spare = layout.spare
    grads = other is not None

    def body(row_ref, col_ref, *refs):
        parts = refs[:count]
        refs = refs[count:]
        if grads:
            other_ref, refs = refs[0], refs[1:]
        weights, keep, send = refs[:3]
        refs = refs[3:]
        if grads:
            grad, full, other_full, total = refs
        else:
            whole, sums, full, total = refs
        step = pl.program_id(0)

        @pl.when(step == 0)
        def _():
            gather_hidden(lax.axis_index("row"), parts, full)
            if spare:
                full[hidden_blocks] = jnp.zeros((tokens, BLK), BF16)
            if grads:
                other_full[pl.ds(0, model_blocks)] = other_ref[...]
                if spare:
                    other_full[model_blocks] = jnp.zeros((tokens, BLK), BF16)
            total[...] = jnp.zeros_like(total)

        work = add_forward if forward else add_backward
        work(layout, row_ref, col_ref, step * here, here, full, weights, total)
        if grads:
            block_products(layout, row_ref, col_ref, step * here, here, full, other_full, grad)

        @pl.when(step == steps - 1)
        def _():
            me = lax.axis_index("col")
            for entry in range(half):
                mine = pl.multiple_of((me ^ (2 * entry)) * piece, piece)
                theirs = pl.multiple_of((me ^ (2 * entry + 1)) * piece, piece)
                for block in range(model_blocks):
                    lanes = pl.ds(block * BLK, BLK)
                    keep[entry, :, lanes] = total[block, pl.ds(mine, piece), :]
                    send[entry, :, lanes] = total[block, pl.ds(theirs, piece), :].astype(BF16)
            if not grads:
                whole[...] = full[pl.ds(0, hidden_blocks)]
                for block in range(hidden_blocks):
                    sums[pl.ds(block, 1), :] = jnp.sum(full[block].astype(F32), axis=0, keepdims=True)

    pair = (half, piece, model_blocks * BLK)
    outs = [shape_of(pair, F32), shape_of(pair, BF16)]
    out_specs = [whole_spec(pair), whole_spec(pair)]
    in_specs = [SM, SM] + [whole_spec(shares[0].shape)] * count
    args = [*rows_cols, *shares]
    scratch = [pltpu.VMEM((hidden_blocks + spare, tokens, BLK), BF16)]
    flops, moved = apply_cost(layout, tokens)
    if grads:
        in_specs += [whole_spec(other.shape)]
        args += [other]
        outs += [shape_of((layout.capacity, BLK, BLK), F32)]
        out_specs += [weight_spec(layout, steps)]
        scratch += [pltpu.VMEM((model_blocks + spare, tokens, BLK), BF16)]
        flops, moved = 2 * flops, 3 * moved
    else:
        outs += [shape_of((hidden_blocks, tokens, BLK), BF16), shape_of((hidden_blocks, BLK), F32)]
        out_specs += [whole_spec(out.shape) for out in outs[2:]]
    scratch += [pltpu.VMEM((model_blocks + spare, tokens, BLK), F32)]
    return call(
        body,
        outs,
        in_specs + [weight_spec(layout, steps)],
        args + [blocks],
        scratch=scratch,
        grid=(steps,),
        out_specs=out_specs,
        flops=flops,
        moved=moved,
    )


def weight_grad(layout, rows_cols, left, right):
    steps = steps_for(layout)
    here = layout.groups // steps
    spare = layout.spare

    def body(row_ref, col_ref, left_ref, right_ref, grad, *held):
        step = pl.program_id(0)
        if spare:

            @pl.when(step == 0)
            def _():
                for source, full in zip((left_ref, right_ref), held):
                    full[pl.ds(0, source.shape[0])] = source[...]
                    full[source.shape[0]] = jnp.zeros(source.shape[1:], BF16)

            left_ref, right_ref = held
        block_products(layout, row_ref, col_ref, step * here, here, left_ref, right_ref, grad)

    flops, moved = apply_cost(layout, left.shape[1])
    return call(
        body,
        [shape_of((layout.capacity, BLK, BLK), F32)],
        [SM, SM, whole_spec(left.shape), whole_spec(right.shape)],
        [*rows_cols, left, right],
        scratch=[pltpu.VMEM((a.shape[0] + 1, *a.shape[1:]), BF16) for a in (left, right)] if spare else [],
        grid=(steps,),
        out_specs=[weight_spec(layout, steps)],
        flops=flops,
        moved=2 * moved,
    )[0]


def add_up(own_ref, parts):
    total = own_ref[...]
    for part in parts:
        total = total + part[...].astype(F32)
    return total


def activate(own, parts, bias):
    def body(own_ref, bias_ref, *refs):
        parts, (value_ref, slope_ref) = refs[:-2], refs[-2:]
        hidden = add_up(own_ref, parts) + bias_ref[...][:, None, :]
        value, slope = gelu_parts(hidden)
        value_ref[...] = value.astype(BF16)
        slope_ref[...] = slope

    outs = [shape_of(own.shape, BF16), shape_of(own.shape, F32)]
    return call(body, outs, [VM] * (2 + len(parts)), [own, bias, *parts], moved=own.size * 20)


def scale_by_slope(own, parts, slope):
    def body(own_ref, slope_ref, *refs):
        parts, out_ref = refs[:-1], refs[-1]
        out_ref[...] = (add_up(own_ref, parts) * slope_ref[...]).astype(BF16)

    outs = [shape_of(own.shape, BF16)]
    return call(body, outs, [VM] * (2 + len(parts)), [own, slope, *parts], moved=own.size * 16)[0]


def pair_sum(keep, came):
    half, piece, width = keep.shape

    def body(keep_ref, came_ref, own_ref, *sends):
        own_ref[...] = keep_ref[0] + came_ref[0].astype(F32)
        for entry, send in enumerate(sends, 1):
            send[...] = (keep_ref[entry] + came_ref[entry].astype(F32)).astype(BF16)

    outs = [shape_of((piece, width), F32)] + [shape_of((piece, width), BF16)] * (half - 1)
    own, *sends = call(body, outs, [VM, VM], [keep, came], moved=keep.size * 8)
    return own, sends


def final_sum(own, parts):
    def body(own_ref, *refs):
        refs[-1][...] = add_up(own_ref, refs[:-1]).astype(BF16)

    outs = [shape_of(own.shape, BF16)]
    return call(body, outs, [VM] * (1 + len(parts)), [own, *parts], moved=own.size * 8)[0]


def gather_col(shard, n_col):
    shards = [None] * n_col
    shards[0] = shard
    for mask in range(2, n_col, 2):
        shards[mask] = swap(shard, "col", n_col, mask)
    for mask in range(0, n_col, 2):
        shards[mask + 1] = swap(shards[mask], "col", n_col, 1)
    return shards


def gather_row(share, n_row):
    return [share] + [swap(share, "row", n_row, mask) for mask in range(1, n_row)]


def send_row(sends, n_row):
    return [swap(send, "row", n_row, mask) for mask, send in enumerate(sends, 1)]


def reduce_col(keep, send, n_col):
    came = swap(send, "col", n_col, 1)
    own, sends = pair_sum(keep, came)
    return own, [swap(part, "col", n_col, 2 * entry) for entry, part in enumerate(sends, 1)]


def local(n_row, n_col, tokens, cotangent, w1_mask, w1_blocks, bias, w2_mask, w2_blocks):
    first_blocks = w1_blocks[0, 0]
    second_blocks = w2_blocks[0, 0]
    model_blocks, hidden_blocks = w1_mask.shape
    first = Slots(w1_mask.shape, first_blocks.shape[0])
    second = Slots(w2_mask.shape, second_blocks.shape[0])
    first_at, second_at = slot_indices([first, second], [w1_mask, w2_mask])
    bias_wide = bias.astype(F32).reshape(hidden_blocks, BLK)

    token_shards = gather_col(tokens, n_col)
    cotangent_shards = gather_col(cotangent, n_col)

    hidden_own, hidden_sends, full_tokens = model_to_hidden(
        first, first_at, token_shards, first_blocks, True, hidden_blocks, n_row
    )
    hidden_parts = send_row(hidden_sends, n_row)
    act_own, act_sends, full_cotangent = model_to_hidden(
        second, second_at, cotangent_shards, second_blocks, False, hidden_blocks, n_row
    )
    act_parts = send_row(act_sends, n_row)

    activated, slope = activate(hidden_own, hidden_parts, bias_wide)
    activated_shares = gather_row(activated, n_row)
    grad_hidden = scale_by_slope(act_own, act_parts, slope)
    grad_shares = gather_row(grad_hidden, n_row)

    out_keep, out_send, w2_grad = hidden_to_model(
        second, second_at, activated_shares, second_blocks, True, model_blocks, n_col, full_cotangent
    )
    out_own, out_parts = reduce_col(out_keep, out_send, n_col)
    in_keep, in_send, full_grad, bias_sum = hidden_to_model(
        first, first_at, grad_shares, first_blocks, False, model_blocks, n_col
    )
    in_own, in_parts = reduce_col(in_keep, in_send, n_col)
    w1_grad = weight_grad(first, first_at, full_tokens, full_grad)
    return (
        final_sum(out_own, out_parts),
        final_sum(in_own, in_parts),
        w1_grad[None, None],
        w2_grad[None, None],
        bias_sum.reshape(-1),
    )


def solution(mesh):
    n_row, n_col = mesh.shape["row"], mesh.shape["col"]
    return jax.shard_map(
        lambda *args: local(n_row, n_col, *args),
        mesh=mesh,
        in_specs=(
            P("col", "row"),
            P("col", "row"),
            P("row", "col"),
            P("row", "col", None, None, None),
            P("col"),
            P("col", "row"),
            P("row", "col", None, None, None),
        ),
        out_specs=(
            P("col", "row"),
            P("col", "row"),
            P("row", "col", None, None, None),
            P("row", "col", None, None, None),
            P("col"),
        ),
        check_vma=False,
    )
```

```python
import math

import jax
import jax.numpy as jnp
from jax import lax
from jax.experimental import pallas as pl
from jax.experimental.pallas import tpu as pltpu
from jax.sharding import PartitionSpec as P

BLK = 128
F32 = jnp.float32
BF16 = jnp.bfloat16
VMEM_LIMIT = 12 * 1024 * 1024
VMEM_GRAD = 28 * 1024 * 1024
RING = 24
FETCH_PARTS = (6, 4, 3, 2, 1)
GRAD_PARTS = (24, 16, 12, 8, 6, 4, 3, 2, 1)

slope_const = math.sqrt(2.0 / math.pi)


def gelu_parts(values):
    inner = slope_const * (values + 0.044715 * values * values * values)
    tangent = jnp.tanh(inner)
    value = 0.5 * values * (1.0 + tangent)
    slope = 0.5 * (1.0 + tangent) + 0.5 * values * (1.0 - tangent * tangent) * slope_const * (
        1.0 + 3.0 * 0.044715 * values * values
    )
    return value, slope


def swap(array, axis, size, mask):
    return lax.ppermute(array, axis, [(place, place ^ mask) for place in range(size)])


def call(body, outs, in_specs, args, scratch=(), grid=None, out_specs=None, flops=0, moved=0, limit=VMEM_LIMIT):
    whole = pl.BlockSpec(memory_space=pltpu.VMEM)
    extra = {} if grid is None else {"grid": grid}
    return pl.pallas_call(
        body,
        out_shape=outs,
        in_specs=in_specs,
        out_specs=[whole] * len(outs) if out_specs is None else out_specs,
        scratch_shapes=list(scratch),
        compiler_params=pltpu.CompilerParams(vmem_limit_bytes=limit),
        cost_estimate=pl.CostEstimate(flops=flops, bytes_accessed=moved, transcendentals=0),
        **extra,
    )(*args)


VM = pl.BlockSpec(memory_space=pltpu.VMEM)
SM = pl.BlockSpec(memory_space=pltpu.SMEM)


def shape_of(shape, dtype):
    return jax.ShapeDtypeStruct(shape, dtype)


def dot(left, right, left_dim, right_dim):
    return lax.dot_general(
        left, right, (((left_dim,), (right_dim,)), ((), ())), preferred_element_type=F32
    )


class Slots:
    def __init__(self, mask_shape, capacity):
        self.rows, self.cols = mask_shape
        self.capacity = capacity
        self.even = self.cols % 8 == 0 and self.cols // 4 <= BLK and capacity == self.rows * (self.cols // 4)
        self.group = self.cols // 4 if self.even else 1
        self.groups = capacity // self.group
        self.spare = 0 if self.even else 1

    def index_args(self, mask):
        flat = mask.reshape(-1)
        count = flat.shape[0]
        places = jnp.arange(count, dtype=jnp.int32)
        lane = jnp.arange(self.cols, dtype=jnp.int32)
        within = jnp.sum(jnp.where(lane[None, :] <= lane[:, None], mask[:, None, :], 0), axis=2)
        row_sum = jnp.sum(mask, axis=1)
        line = jnp.arange(self.rows, dtype=jnp.int32)
        before = jnp.sum(jnp.where(line[None, :] < line[:, None], row_sum[None, :], 0), axis=1)
        rank = (within + before[:, None] - 1).reshape(-1)
        slot = jnp.arange(self.capacity, dtype=jnp.int32)
        hit = (rank[None, :] == slot[:, None]) & (flat[None, :] > 0)
        order = jnp.sum(jnp.where(hit, places[None, :], 0), axis=1)
        live = slot < jnp.sum(flat)
        row = jnp.where(live, order // self.cols, self.rows)
        col = jnp.where(live, order % self.cols, self.cols)
        return row, col


def index_kernel(layout, mask_ref, out_ref):
    rows, cols, group = layout.rows, layout.cols, layout.group
    mask = mask_ref[...].astype(F32)
    lower = lax.broadcasted_iota(jnp.int32, (cols, cols), 0)
    upper = lax.broadcasted_iota(jnp.int32, (cols, cols), 1)
    ramp = jnp.where(lower <= upper, 1.0, 0.0).astype(BF16)
    rank = dot(mask.astype(BF16), ramp, 1, 0)
    place = lax.broadcasted_iota(jnp.int32, (rows, cols), 1).astype(F32)
    lane = lax.broadcasted_iota(jnp.int32, (rows, BLK), 1)
    found = jnp.zeros((rows, BLK), F32)
    for slot in range(group):
        hit = (rank == float(slot + 1)) & (mask > 0.0)
        column = jnp.sum(jnp.where(hit, place, 0.0), axis=1, keepdims=True)
        found = jnp.where(lane == slot, column, found)
    out_ref[...] = found.astype(jnp.int32)


def slot_indices(layout, mask):
    if layout.even:
        out = call(
            lambda mask_ref, out_ref: index_kernel(layout, mask_ref, out_ref),
            [shape_of((layout.rows, BLK), jnp.int32)],
            [VM],
            [mask],
        )[0]
        return out, out
    return layout.index_args(mask)


def read_slot(layout, row_ref, col_ref, group, member):
    if layout.even:
        return group, col_ref[group, member]
    return row_ref[group], col_ref[group]


def add_forward(layout, row_ref, col_ref, first, here, source, blocks, total):
    group = layout.group
    for near in range(here):
        if layout.even:
            left = source[first + near]
            width = 2 if group % 2 == 0 else 1
            for member in range(0, group, width):
                place = near * group + member
                right = [blocks[place + more] for more in range(width)]
                right = right[0] if width == 1 else jnp.concatenate(right, axis=1)
                product = dot(left, right, 1, 0)
                for more in range(width):
                    col = col_ref[first + near, member + more]
                    total[col] += product[:, more * BLK : (more + 1) * BLK]
        else:
            row, col = read_slot(layout, row_ref, col_ref, first + near, 0)
            total[col] += dot(source[row], blocks[near], 1, 0)


def add_backward(layout, row_ref, col_ref, first, here, source, blocks, total):
    group = layout.group
    for near in range(here):
        if layout.even:
            width = 2 if group % 2 == 0 else 1
            result = None
            for member in range(0, group, width):
                place = near * group + member
                cols = [col_ref[first + near, member + more] for more in range(width)]
                left = [source[col] for col in cols]
                right = [blocks[place + more] for more in range(width)]
                left = left[0] if width == 1 else jnp.concatenate(left, axis=1)
                right = right[0] if width == 1 else jnp.concatenate(right, axis=1)
                product = dot(left, right, 1, 1)
                result = product if result is None else result + product
            total[first + near] = result
        else:
            row, col = read_slot(layout, row_ref, col_ref, first + near, 0)
            total[row] += dot(source[col], blocks[near], 1, 1)


def block_products(layout, row_ref, col_ref, first, here, left, right, out):
    group = layout.group
    for near in range(here):
        if layout.even:
            turned = left[first + near].T
            width = 2 if group % 2 == 0 else 1
            for member in range(0, group, width):
                place = near * group + member
                cols = [col_ref[first + near, member + more] for more in range(width)]
                wide = [right[col] for col in cols]
                wide = wide[0] if width == 1 else jnp.concatenate(wide, axis=1)
                product = dot(turned, wide, 1, 0)
                for more in range(width):
                    out[place + more] = product[:, more * BLK : (more + 1) * BLK]
        else:
            row, col = read_slot(layout, row_ref, col_ref, first + near, 0)
            live = row < layout.rows
            product = dot(left[row].T, right[col], 1, 0)
            out[near] = jnp.where(live, product, 0.0)


def gather_model(me, shards, which, stage, full):
    piece = shards[0].shape[1]
    for mask, shard in enumerate(shards):
        start = pl.multiple_of((me ^ mask) * piece, piece)
        stage[pl.ds(start, piece), :] = shard[which].astype(F32)
    for block in range(shards[0].shape[2] // BLK):
        full[block] = stage[:, block * BLK : (block + 1) * BLK].astype(full.dtype)


def gather_hidden(me, shares, full):
    blocks, piece, _ = shares[0].shape
    for mask, share in enumerate(shares):
        start = pl.multiple_of((me ^ mask) * piece, piece)
        full[pl.ds(0, blocks), pl.ds(start, piece), :] = share[...]


def parts_of(layout, choices):
    parts = next(parts for parts in choices if layout.groups % parts == 0)
    return parts, layout.groups // parts, layout.capacity // parts


def apply_cost(layout, tokens):
    return 2 * layout.capacity * BLK * BLK * tokens, 2 * layout.capacity * BLK * BLK


def together(first, second):
    def body(first_ref, second_ref, out_ref):
        out_ref[0] = first_ref[...]
        out_ref[1] = second_ref[...]

    block = pl.BlockSpec(first.shape, lambda step: (0, 0))
    return call(
        body,
        [shape_of((2, *first.shape), first.dtype)],
        [block, block],
        [pltpu.with_memory_space_constraint(array, pltpu.HBM) for array in (first, second)],
        grid=(1,),
        moved=8 * first.size,
    )[0]


def model_to_hidden(layout, rows_cols, shards, which, blocks, forward, hidden_blocks, n_row, after=()):
    count = len(shards)
    _, part, width = shards[0].shape
    tokens = part * count
    model_blocks = width // BLK
    piece = tokens // n_row
    spare = layout.spare
    parts, here, size = parts_of(layout, FETCH_PARTS)

    def body(row_ref, col_ref, *refs):
        shard_refs = refs[:count]
        weights, own, *sends, whole, held, stage, full, total, done = refs[count + len(after) :]
        places = [pl.ds(part * size, size) for part in range(parts)]
        copies = [
            pltpu.make_async_copy(weights.at[place], held.at[place], done.at[part])
            for part, place in enumerate(places)
        ]
        for copy in copies:
            copy.start()
        gather_model(lax.axis_index("col"), shard_refs, which, stage, full)
        if spare:
            full[model_blocks] = jnp.zeros((tokens, BLK), BF16)
        if forward or spare:
            total[...] = jnp.zeros_like(total)
        whole[...] = full[pl.ds(0, model_blocks)]
        work = add_forward if forward else add_backward
        for part, place in enumerate(places):
            copies[part].wait()
            work(layout, row_ref, col_ref, part * here, here, full, held.at[place], total)
        me = lax.axis_index("row")
        for mask, out in enumerate([own] + sends):
            start = pl.multiple_of((me ^ mask) * piece, piece)
            out[...] = total[pl.ds(0, hidden_blocks), pl.ds(start, piece), :].astype(out.dtype)

    share = (hidden_blocks, piece, BLK)
    outs = [shape_of(share, F32)] + [shape_of(share, BF16)] * (n_row - 1)
    outs += [shape_of((model_blocks, tokens, BLK), BF16), pltpu.VMEM(blocks.shape, blocks.dtype)]
    flops, moved = apply_cost(layout, tokens)
    args = [*rows_cols, *shards, *after, pltpu.with_memory_space_constraint(blocks, pltpu.HBM)]
    own, *sends, whole, held = call(
        body,
        outs,
        [SM, SM] + [VM] * (len(args) - 3) + [pl.BlockSpec(memory_space=pltpu.HBM)],
        args,
        scratch=[
            pltpu.VMEM((tokens, width), F32),
            pltpu.VMEM((model_blocks + spare, tokens, BLK), BF16),
            pltpu.VMEM((hidden_blocks + spare, tokens, BLK), F32),
            pltpu.SemaphoreType.DMA((parts,)),
        ],
        flops=flops,
        moved=moved,
    )
    return own, sends, whole, held


def hidden_to_model(layout, rows_cols, shares, blocks, forward, model_blocks, n_col, other=None, after=()):
    count = len(shares)
    hidden_blocks, part, _ = shares[0].shape
    tokens = part * count
    piece = tokens // n_col
    half = n_col // 2
    spare = layout.spare
    grads = other is not None

    def body(row_ref, col_ref, *refs):
        share_refs, refs = refs[:count], refs[count + len(after) :]
        if grads:
            other_ref, weights, keep, send, token, grad, full, total, other_full, made, done = refs
            token[...] = jnp.zeros_like(token)
        else:
            weights, keep, send, full, total = refs
        gather_hidden(lax.axis_index("row"), share_refs, full)
        if spare:
            full[hidden_blocks] = jnp.zeros((tokens, BLK), BF16)
        if forward or spare:
            total[...] = jnp.zeros_like(total)
        if grads:
            if spare:
                other_full[pl.ds(0, model_blocks)] = other_ref[...]
                other_full[model_blocks] = jnp.zeros((tokens, BLK), BF16)
                other_ref = other_full
            copies = send_products(layout, row_ref, col_ref, full, other_ref, made, grad, done)
        work = add_forward if forward else add_backward
        work(layout, row_ref, col_ref, 0, layout.groups, full, weights, total)
        me = lax.axis_index("col")
        for entry in range(half):
            mine = pl.multiple_of((me ^ (2 * entry)) * piece, piece)
            theirs = pl.multiple_of((me ^ (2 * entry + 1)) * piece, piece)
            for block in range(model_blocks):
                lanes = pl.ds(block * BLK, BLK)
                keep[entry, :, lanes] = total[block, pl.ds(mine, piece), :]
                send[entry, :, lanes] = total[block, pl.ds(theirs, piece), :].astype(BF16)
        if grads:
            for copy in copies:
                copy.wait()

    pair = (half, piece, model_blocks * BLK)
    outs = [shape_of(pair, F32), shape_of(pair, BF16)]
    out_specs = [VM] * (4 if grads else 2)
    args = [*rows_cols, *shares, *after]
    scratch = [
        pltpu.VMEM((hidden_blocks + spare, tokens, BLK), BF16),
        pltpu.VMEM((model_blocks + spare, tokens, BLK), F32),
    ]
    flops, moved = apply_cost(layout, tokens)
    if grads:
        outs += [shape_of((8, BLK), F32), shape_of((layout.capacity, BLK, BLK), F32)]
        out_specs[3] = pl.BlockSpec(memory_space=pltpu.HBM)
        args += [other]
        scratch += [
            pltpu.VMEM((model_blocks + spare, tokens, BLK), BF16),
            *ring_scratch(layout),
        ]
        flops, moved = 2 * flops, 3 * moved
    args += [pltpu.with_memory_space_constraint(blocks, pltpu.VMEM)]
    return call(
        body,
        outs,
        [SM, SM] + [VM] * (len(args) - 2),
        args,
        scratch=scratch,
        out_specs=out_specs,
        flops=flops,
        moved=moved,
        limit=VMEM_GRAD if grads else VMEM_LIMIT,
    )


def ring_scratch(layout):
    parts, _, size = parts_of(layout, GRAD_PARTS)
    slots = min(RING, parts)
    return [pltpu.VMEM((slots, size, BLK, BLK), F32), pltpu.SemaphoreType.DMA((slots,))]


def send_products(layout, row_ref, col_ref, left, right, ring, grad, done):
    parts, here, size = parts_of(layout, GRAD_PARTS)
    slots = ring.shape[0]
    copies = []
    for part in range(parts):
        slot = part % slots
        if part >= slots:
            copies[part - slots].wait()
        block_products(layout, row_ref, col_ref, part * here, here, left, right, ring.at[slot])
        place = pl.ds(part * size, size)
        copies.append(pltpu.make_async_copy(ring.at[slot], grad.at[place], done.at[slot]))
        copies[-1].start()
    return copies[-slots:]


def weight_grad(layout, rows_cols, left, shares):
    spare = layout.spare
    count = len(shares)
    left_blocks, tokens, _ = left.shape
    hidden_blocks = shares[0].shape[0]

    def body(row_ref, col_ref, left_ref, *refs):
        share_refs, (grad, sum_ref, made, done, full, *wide) = refs[:count], refs[count:]
        gather_hidden(lax.axis_index("row"), share_refs, full)
        if spare:
            full[hidden_blocks] = jnp.zeros((tokens, BLK), BF16)
            wide[0][pl.ds(0, left_blocks)] = left_ref[...]
            wide[0][left_blocks] = jnp.zeros((tokens, BLK), BF16)
            left_ref = wide[0]
        copies = send_products(layout, row_ref, col_ref, left_ref, full, made, grad, done)
        for block in range(hidden_blocks):
            sum_ref[pl.ds(block, 1), :] = jnp.sum(full[block].astype(F32), axis=0, keepdims=True)
        for copy in copies:
            copy.wait()

    flops, moved = apply_cost(layout, tokens)
    out = shape_of((layout.capacity, BLK, BLK), F32)
    scratch = ring_scratch(layout)
    scratch += [pltpu.VMEM((hidden_blocks + spare, tokens, BLK), BF16)]
    if spare:
        scratch += [pltpu.VMEM((left_blocks + 1, tokens, BLK), BF16)]
    return call(
        body,
        [out, shape_of((hidden_blocks, BLK), F32)],
        [SM, SM, VM] + [VM] * count,
        [*rows_cols, left, *shares],
        scratch=scratch,
        out_specs=[pl.BlockSpec(memory_space=pltpu.HBM), VM],
        flops=flops,
        moved=2 * moved,
        limit=VMEM_GRAD,
    )


def add_up(own_ref, parts):
    total = own_ref[...]
    for part in parts:
        total = total + part[...].astype(F32)
    return total


def activate(own, parts, bias):
    def body(own_ref, bias_ref, *refs):
        parts, (value_ref, slope_ref) = refs[:-2], refs[-2:]
        hidden = add_up(own_ref, parts) + bias_ref[...][:, None, :]
        value, slope = gelu_parts(hidden)
        value_ref[...] = value.astype(BF16)
        slope_ref[...] = slope

    outs = [shape_of(own.shape, BF16), shape_of(own.shape, F32)]
    return call(body, outs, [VM] * (2 + len(parts)), [own, bias, *parts], moved=own.size * 20)


def scale_by_slope(own, parts, slope):
    def body(own_ref, slope_ref, *refs):
        parts, out_ref = refs[:-1], refs[-1]
        out_ref[...] = (add_up(own_ref, parts) * slope_ref[...]).astype(BF16)

    outs = [shape_of(own.shape, BF16)]
    return call(body, outs, [VM] * (2 + len(parts)), [own, slope, *parts], moved=own.size * 16)[0]


def pair_sums(*pairs):
    half, piece, width = pairs[0][0].shape
    count = len(pairs)

    def body(*refs):
        sources, owns, sends = refs[: 2 * count], refs[2 * count : 3 * count], refs[3 * count :]
        for which in range(count):
            keep, came = sources[2 * which : 2 * which + 2]
            owns[which][...] = keep[0] + came[0].astype(F32)
            for entry, send in enumerate(sends, 1):
                send[which] = (keep[entry] + came[entry].astype(F32)).astype(BF16)

    outs = [shape_of((piece, width), F32)] * count + [shape_of((count, piece, width), BF16)] * (half - 1)
    args = [array for pair in pairs for array in pair]
    results = call(body, outs, [VM] * len(args), args, moved=8 * count * half * piece * width)
    return results[:count], results[count:]


def final_sums(owns, parts):
    def body(*refs):
        sources, came, outs = refs[: len(owns)], refs[len(owns) : -len(owns)], refs[-len(owns) :]
        for which, (own, out) in enumerate(zip(sources, outs)):
            total = own[...]
            for part in came:
                total = total + part[which].astype(F32)
            out[...] = total.astype(BF16)

    outs = [shape_of(own.shape, BF16) for own in owns]
    return call(body, outs, [VM] * (len(owns) + len(parts)), [*owns, *parts], moved=8 * sum(own.size for own in owns))


def gather_col(shard, n_col):
    shards = [None] * n_col
    shards[0] = shard
    for mask in range(2, n_col, 2):
        shards[mask] = swap(shard, "col", n_col, mask)
    for mask in range(0, n_col, 2):
        shards[mask + 1] = swap(shards[mask], "col", n_col, 1)
    return shards


def gather_row(share, n_row):
    return [share] + [swap(share, "row", n_row, mask) for mask in range(1, n_row)]


def send_row(sends, n_row):
    return [swap(send, "row", n_row, mask) for mask, send in enumerate(sends, 1)]


def local(n_row, n_col, tokens, cotangent, w1_mask, w1_blocks, bias, w2_mask, w2_blocks):
    first_blocks = w1_blocks[0, 0]
    second_blocks = w2_blocks[0, 0]
    model_blocks, hidden_blocks = w1_mask.shape
    first = Slots(w1_mask.shape, first_blocks.shape[0])
    second = Slots(w2_mask.shape, second_blocks.shape[0])
    first_at, second_at = slot_indices(first, w1_mask), slot_indices(second, w2_mask)
    bias_wide = bias.astype(F32).reshape(hidden_blocks, BLK)

    shards = gather_col(together(tokens, cotangent), n_col)

    hidden_own, hidden_sends, full_tokens, first_held = model_to_hidden(
        first, first_at, shards, 0, first_blocks, True, hidden_blocks, n_row
    )
    hidden_parts = send_row(hidden_sends, n_row)
    act_own, act_sends, full_cotangent, second_held = model_to_hidden(
        second, second_at, shards, 1, second_blocks, False, hidden_blocks, n_row, after=(full_tokens,)
    )
    act_parts = send_row(act_sends, n_row)

    activated, slope = activate(hidden_own, hidden_parts, bias_wide)
    activated_shares = gather_row(activated, n_row)
    grad_hidden = scale_by_slope(act_own, act_parts, slope)
    grad_shares = gather_row(grad_hidden, n_row)

    out_keep, out_send, out_done, w2_grad = hidden_to_model(
        second, second_at, activated_shares, second_held, True, model_blocks, n_col, other=full_cotangent
    )
    out_came = swap(out_send, "col", n_col, 1)
    in_keep, in_send = hidden_to_model(
        first, first_at, grad_shares, first_held, False, model_blocks, n_col, after=(out_done,)
    )
    in_came = swap(in_send, "col", n_col, 1)
    owns, sends = pair_sums((out_keep, out_came), (in_keep, in_came))
    parts = [swap(send, "col", n_col, 2 * entry) for entry, send in enumerate(sends, 1)]
    w1_grad, bias_sum = weight_grad(first, first_at, full_tokens, grad_shares)
    out, tokens_grad = final_sums(owns, parts)
    return (
        out,
        tokens_grad,
        w1_grad[None, None],
        w2_grad[None, None],
        bias_sum.reshape(-1),
    )


def solution(mesh):
    n_row, n_col = mesh.shape["row"], mesh.shape["col"]
    return jax.shard_map(
        lambda *args: local(n_row, n_col, *args),
        mesh=mesh,
        in_specs=(
            P("col", "row"),
            P("col", "row"),
            P("row", "col"),
            P("row", "col", None, None, None),
            P("col"),
            P("col", "row"),
            P("row", "col", None, None, None),
        ),
        out_specs=(
            P("col", "row"),
            P("col", "row"),
            P("row", "col", None, None, None),
            P("row", "col", None, None, None),
            P("col"),
        ),
        check_vma=False,
    )
```

```python
import math

import jax
import jax.numpy as jnp
from jax import lax
from jax.experimental import pallas as pl
from jax.experimental.pallas import tpu as pltpu
from jax.sharding import PartitionSpec as P

BLK = 128
F32 = jnp.float32
BF16 = jnp.bfloat16
VMEM_LIMIT = 12 * 1024 * 1024
VMEM_GRAD = 28 * 1024 * 1024
RING = 24
GRAD_PARTS = (24, 16, 12, 8, 6, 4, 3, 2, 1)

slope_const = math.sqrt(2.0 / math.pi)


def gelu_parts(values):
    inner = slope_const * (values + 0.044715 * values * values * values)
    tangent = jnp.tanh(inner)
    value = 0.5 * values * (1.0 + tangent)
    slope = 0.5 * (1.0 + tangent) + 0.5 * values * (1.0 - tangent * tangent) * slope_const * (
        1.0 + 3.0 * 0.044715 * values * values
    )
    return value, slope


def swap(array, axis, size, mask):
    return lax.ppermute(array, axis, [(place, place ^ mask) for place in range(size)])


def call(body, outs, in_specs, args, scratch=(), grid=None, out_specs=None, flops=0, moved=0, limit=VMEM_LIMIT):
    whole = pl.BlockSpec(memory_space=pltpu.VMEM)
    extra = {} if grid is None else {"grid": grid}
    return pl.pallas_call(
        body,
        out_shape=outs,
        in_specs=in_specs,
        out_specs=[whole] * len(outs) if out_specs is None else out_specs,
        scratch_shapes=list(scratch),
        compiler_params=pltpu.CompilerParams(vmem_limit_bytes=limit),
        cost_estimate=pl.CostEstimate(flops=flops, bytes_accessed=moved, transcendentals=0),
        **extra,
    )(*args)


VM = pl.BlockSpec(memory_space=pltpu.VMEM)
SM = pl.BlockSpec(memory_space=pltpu.SMEM)


def shape_of(shape, dtype):
    return jax.ShapeDtypeStruct(shape, dtype)


def dot(left, right, left_dim, right_dim):
    return lax.dot_general(
        left, right, (((left_dim,), (right_dim,)), ((), ())), preferred_element_type=F32
    )


class Slots:
    def __init__(self, mask_shape, capacity):
        self.rows, self.cols = mask_shape
        self.capacity = capacity
        self.even = self.cols % 8 == 0 and self.cols // 4 <= BLK and capacity == self.rows * (self.cols // 4)
        self.group = self.cols // 4 if self.even else 1
        self.groups = capacity // self.group
        self.spare = 0 if self.even else 1

    def uneven_slots(self, mask):
        self.even, self.group, self.groups, self.spare = False, 1, self.capacity, 1
        flat = mask.reshape(-1)
        count = flat.shape[0]
        places = jnp.arange(count, dtype=jnp.int32)
        lane = jnp.arange(self.cols, dtype=jnp.int32)
        within = jnp.sum(jnp.where(lane[None, :] <= lane[:, None], mask[:, None, :], 0), axis=2)
        row_sum = jnp.sum(mask, axis=1)
        line = jnp.arange(self.rows, dtype=jnp.int32)
        before = jnp.sum(jnp.where(line[None, :] < line[:, None], row_sum[None, :], 0), axis=1)
        rank = (within + before[:, None] - 1).reshape(-1)
        slot = jnp.arange(self.capacity, dtype=jnp.int32)
        hit = (rank[None, :] == slot[:, None]) & (flat[None, :] > 0)
        order = jnp.sum(jnp.where(hit, places[None, :], 0), axis=1)
        live = slot < jnp.sum(flat)
        row = jnp.where(live, order // self.cols, self.rows)
        col = jnp.where(live, order % self.cols, self.cols)
        return row, col


def index_kernel(layout, mask, out_ref):
    rows, cols, group = layout.rows, layout.cols, layout.group
    lower = lax.broadcasted_iota(jnp.int32, (cols, cols), 0)
    upper = lax.broadcasted_iota(jnp.int32, (cols, cols), 1)
    ramp = jnp.where(lower <= upper, 1.0, 0.0).astype(BF16)
    rank = dot(mask.astype(BF16), ramp, 1, 0)
    place = lax.broadcasted_iota(jnp.int32, (rows, cols), 1).astype(F32)
    lane = lax.broadcasted_iota(jnp.int32, (rows, BLK), 1)
    found = jnp.zeros((rows, BLK), F32)
    for slot in range(group):
        hit = (rank == float(slot + 1)) & (mask > 0.0)
        column = jnp.sum(jnp.where(hit, place, 0.0), axis=1, keepdims=True)
        found = jnp.where(lane == slot, column, found)
    out_ref[...] = found.astype(jnp.int32)


def slot_indices(layouts, masks):
    if not all(layout.even for layout in layouts):
        return [layout.uneven_slots(mask) for layout, mask in zip(layouts, masks)]
    turned = [layout.rows > layout.cols for layout in layouts]
    arrays = [mask.T if turn else mask for mask, turn in zip(masks, turned)]

    def body(*refs):
        for which, (layout, turn) in enumerate(zip(layouts, turned)):
            mask = refs[which][...].astype(F32)
            index_kernel(layout, mask.T if turn else mask, refs[len(layouts) + which])

    outs = call(
        body,
        [shape_of((layout.rows, BLK), jnp.int32) for layout in layouts],
        [pl.BlockSpec(array.shape, lambda step: (0, 0)) for array in arrays],
        [pltpu.with_memory_space_constraint(array, pltpu.HBM) for array in arrays],
        grid=(1,),
    )
    return [(out, out) for out in outs]


def read_slot(layout, row_ref, col_ref, group, member):
    if layout.even:
        return group, col_ref[group, member]
    return row_ref[group], col_ref[group]


def add_forward(layout, row_ref, col_ref, first, here, source, blocks, total):
    group = layout.group
    for near in range(here):
        if layout.even:
            left = source[first + near]
            width = 2 if group % 2 == 0 else 1
            for member in range(0, group, width):
                place = near * group + member
                right = [blocks[place + more] for more in range(width)]
                right = right[0] if width == 1 else jnp.concatenate(right, axis=1)
                product = dot(left, right, 1, 0)
                for more in range(width):
                    col = col_ref[first + near, member + more]
                    total[col] += product[:, more * BLK : (more + 1) * BLK]
        else:
            row, col = read_slot(layout, row_ref, col_ref, first + near, 0)
            total[col] += dot(source[row], blocks[near], 1, 0)


def add_backward(layout, row_ref, col_ref, first, here, source, blocks, total):
    group = layout.group
    for near in range(here):
        if layout.even:
            width = 2 if group % 2 == 0 else 1
            result = None
            for member in range(0, group, width):
                place = near * group + member
                cols = [col_ref[first + near, member + more] for more in range(width)]
                left = [source[col] for col in cols]
                right = [blocks[place + more] for more in range(width)]
                left = left[0] if width == 1 else jnp.concatenate(left, axis=1)
                right = right[0] if width == 1 else jnp.concatenate(right, axis=1)
                product = dot(left, right, 1, 1)
                result = product if result is None else result + product
            total[first + near] = result
        else:
            row, col = read_slot(layout, row_ref, col_ref, first + near, 0)
            total[row] += dot(source[col], blocks[near], 1, 1)


def block_products(layout, row_ref, col_ref, first, here, left, right, out):
    group = layout.group
    for near in range(here):
        if layout.even:
            turned = left[first + near].T
            width = 2 if group % 2 == 0 else 1
            for member in range(0, group, width):
                place = near * group + member
                cols = [col_ref[first + near, member + more] for more in range(width)]
                wide = [right[col] for col in cols]
                wide = wide[0] if width == 1 else jnp.concatenate(wide, axis=1)
                product = dot(turned, wide, 1, 0)
                for more in range(width):
                    out[place + more] = product[:, more * BLK : (more + 1) * BLK]
        else:
            row, col = read_slot(layout, row_ref, col_ref, first + near, 0)
            live = row < layout.rows
            product = dot(left[row].T, right[col], 1, 0)
            out[near] = jnp.where(live, product, 0.0)


def gather_model(me, shards, which, stage, full):
    piece = shards[0].shape[1]
    for mask, shard in enumerate(shards):
        start = pl.multiple_of((me ^ mask) * piece, piece)
        stage[pl.ds(start, piece), :] = shard[which].astype(F32)
    for block in range(shards[0].shape[2] // BLK):
        full[block] = stage[:, block * BLK : (block + 1) * BLK].astype(full.dtype)


def gather_hidden(me, shares, full):
    blocks, piece, _ = shares[0].shape
    for mask, share in enumerate(shares):
        start = pl.multiple_of((me ^ mask) * piece, piece)
        full[pl.ds(0, blocks), pl.ds(start, piece), :] = share[...]


def parts_of(layout, choices):
    parts = next(parts for parts in choices if layout.groups % parts == 0)
    return parts, layout.groups // parts, layout.capacity // parts


def apply_cost(layout, tokens):
    return 2 * layout.capacity * BLK * BLK * tokens, 2 * layout.capacity * BLK * BLK


def together(first, second):
    def body(first_ref, second_ref, out_ref):
        out_ref[0] = first_ref[...]
        out_ref[1] = second_ref[...]

    block = pl.BlockSpec(first.shape, lambda step: (0, 0))
    return call(
        body,
        [shape_of((2, *first.shape), first.dtype)],
        [block, block],
        [pltpu.with_memory_space_constraint(array, pltpu.HBM) for array in (first, second)],
        grid=(1,),
        moved=8 * first.size,
    )[0]


def fetch(blocks):
    def body(from_ref, to_ref, token, done):
        copy = pltpu.make_async_copy(from_ref, to_ref, done)
        copy.start()
        token[...] = jnp.zeros_like(token)
        copy.wait()

    return call(
        body,
        [pltpu.VMEM(blocks.shape, blocks.dtype), shape_of((8, BLK), F32)],
        [pl.BlockSpec(memory_space=pltpu.HBM)],
        [pltpu.with_memory_space_constraint(blocks, pltpu.HBM)],
        scratch=[pltpu.SemaphoreType.DMA],
        moved=4 * blocks.size,
    )


def follow(array, *before):
    def body(array_ref, *refs):
        refs[-1][...] = array_ref[...]

    specs = [VM] * (1 + len(before))
    return call(body, [shape_of(array.shape, array.dtype)], specs, [array, *before], moved=4 * array.size)[0]


def model_to_hidden(layout, rows_cols, shards, which, blocks, forward, hidden_blocks, n_row, after=()):
    count = len(shards)
    _, part, width = shards[0].shape
    tokens = part * count
    model_blocks = width // BLK
    piece = tokens // n_row
    spare = layout.spare

    def body(row_ref, col_ref, *refs):
        shard_refs = refs[:count]
        weights, own, *sends, whole, stage, full, total = refs[count + len(after) :]
        gather_model(lax.axis_index("col"), shard_refs, which, stage, full)
        if spare:
            full[model_blocks] = jnp.zeros((tokens, BLK), BF16)
        if forward or spare:
            total[...] = jnp.zeros_like(total)
        work = add_forward if forward else add_backward
        work(layout, row_ref, col_ref, 0, layout.groups, full, weights, total)
        me = lax.axis_index("row")
        for mask, out in enumerate([own] + sends):
            start = pl.multiple_of((me ^ mask) * piece, piece)
            out[...] = total[pl.ds(0, hidden_blocks), pl.ds(start, piece), :].astype(out.dtype)
        whole[...] = full[pl.ds(0, model_blocks)]

    share = (hidden_blocks, piece, BLK)
    outs = [shape_of(share, F32)] + [shape_of(share, BF16)] * (n_row - 1)
    outs += [shape_of((model_blocks, tokens, BLK), BF16)]
    flops, moved = apply_cost(layout, tokens)
    args = [*rows_cols, *shards, *after, pltpu.with_memory_space_constraint(blocks, pltpu.VMEM)]
    own, *sends, whole = call(
        body,
        outs,
        [SM, SM] + [VM] * (len(args) - 2),
        args,
        scratch=[
            pltpu.VMEM((tokens, width), F32),
            pltpu.VMEM((model_blocks + spare, tokens, BLK), BF16),
            pltpu.VMEM((hidden_blocks + spare, tokens, BLK), F32),
        ],
        flops=flops,
        moved=moved,
    )
    return own, sends, whole


def hidden_to_model(layout, rows_cols, shares, blocks, forward, model_blocks, n_col, other=None, after=()):
    count = len(shares)
    hidden_blocks, part, _ = shares[0].shape
    tokens = part * count
    piece = tokens // n_col
    half = n_col // 2
    spare = layout.spare
    grads = other is not None

    def body(row_ref, col_ref, *refs):
        share_refs, refs = refs[:count], refs[count + len(after) :]
        if grads:
            other_ref, weights, keep, send, token, grad, full, total, other_full, made, done = refs
            token[...] = jnp.zeros_like(token)
        else:
            weights, keep, send, full, total = refs
        gather_hidden(lax.axis_index("row"), share_refs, full)
        if spare:
            full[hidden_blocks] = jnp.zeros((tokens, BLK), BF16)
        if forward or spare:
            total[...] = jnp.zeros_like(total)
        if grads:
            if spare:
                other_full[pl.ds(0, model_blocks)] = other_ref[...]
                other_full[model_blocks] = jnp.zeros((tokens, BLK), BF16)
                other_ref = other_full
            copies = send_products(layout, row_ref, col_ref, full, other_ref, made, grad, done)
        work = add_forward if forward else add_backward
        work(layout, row_ref, col_ref, 0, layout.groups, full, weights, total)
        me = lax.axis_index("col")
        for entry in range(half):
            mine = pl.multiple_of((me ^ (2 * entry)) * piece, piece)
            theirs = pl.multiple_of((me ^ (2 * entry + 1)) * piece, piece)
            for block in range(model_blocks):
                lanes = pl.ds(block * BLK, BLK)
                keep[entry, :, lanes] = total[block, pl.ds(mine, piece), :]
                send[entry, :, lanes] = total[block, pl.ds(theirs, piece), :].astype(BF16)
        if grads:
            for copy in copies:
                copy.wait()

    pair = (half, piece, model_blocks * BLK)
    outs = [shape_of(pair, F32), shape_of(pair, BF16)]
    out_specs = [VM] * (4 if grads else 2)
    args = [*rows_cols, *shares, *after]
    scratch = [
        pltpu.VMEM((hidden_blocks + spare, tokens, BLK), BF16),
        pltpu.VMEM((model_blocks + spare, tokens, BLK), F32),
    ]
    flops, moved = apply_cost(layout, tokens)
    if grads:
        outs += [shape_of((8, BLK), F32), shape_of((layout.capacity, BLK, BLK), F32)]
        out_specs[3] = pl.BlockSpec(memory_space=pltpu.HBM)
        args += [other]
        scratch += [
            pltpu.VMEM((model_blocks + spare, tokens, BLK), BF16),
            *ring_scratch(layout),
        ]
        flops, moved = 2 * flops, 3 * moved
    args += [pltpu.with_memory_space_constraint(blocks, pltpu.VMEM)]
    return call(
        body,
        outs,
        [SM, SM] + [VM] * (len(args) - 2),
        args,
        scratch=scratch,
        out_specs=out_specs,
        flops=flops,
        moved=moved,
        limit=VMEM_GRAD if grads else VMEM_LIMIT,
    )


def ring_scratch(layout):
    parts, _, size = parts_of(layout, GRAD_PARTS)
    slots = min(RING, parts)
    return [pltpu.VMEM((slots, size, BLK, BLK), F32), pltpu.SemaphoreType.DMA((slots,))]


def send_products(layout, row_ref, col_ref, left, right, ring, grad, done):
    parts, here, size = parts_of(layout, GRAD_PARTS)
    slots = ring.shape[0]
    copies = []
    for part in range(parts):
        slot = part % slots
        if part >= slots:
            copies[part - slots].wait()
        block_products(layout, row_ref, col_ref, part * here, here, left, right, ring.at[slot])
        place = pl.ds(part * size, size)
        copies.append(pltpu.make_async_copy(ring.at[slot], grad.at[place], done.at[slot]))
        copies[-1].start()
    return copies[-slots:]


def weight_grad(layout, rows_cols, left, shares):
    spare = layout.spare
    count = len(shares)
    left_blocks, tokens, _ = left.shape
    hidden_blocks = shares[0].shape[0]

    def body(row_ref, col_ref, left_ref, *refs):
        share_refs, (grad, sum_ref, made, done, full, *wide) = refs[:count], refs[count:]
        gather_hidden(lax.axis_index("row"), share_refs, full)
        if spare:
            full[hidden_blocks] = jnp.zeros((tokens, BLK), BF16)
            wide[0][pl.ds(0, left_blocks)] = left_ref[...]
            wide[0][left_blocks] = jnp.zeros((tokens, BLK), BF16)
            left_ref = wide[0]
        copies = send_products(layout, row_ref, col_ref, left_ref, full, made, grad, done)
        for block in range(hidden_blocks):
            sum_ref[pl.ds(block, 1), :] = jnp.sum(full[block].astype(F32), axis=0, keepdims=True)
        for copy in copies:
            copy.wait()

    flops, moved = apply_cost(layout, tokens)
    out = shape_of((layout.capacity, BLK, BLK), F32)
    scratch = ring_scratch(layout)
    scratch += [pltpu.VMEM((hidden_blocks + spare, tokens, BLK), BF16)]
    if spare:
        scratch += [pltpu.VMEM((left_blocks + 1, tokens, BLK), BF16)]
    return call(
        body,
        [out, shape_of((hidden_blocks, BLK), F32)],
        [SM, SM, VM] + [VM] * count,
        [*rows_cols, left, *shares],
        scratch=scratch,
        out_specs=[pl.BlockSpec(memory_space=pltpu.HBM), VM],
        flops=flops,
        moved=2 * moved,
        limit=VMEM_GRAD,
    )


def add_up(own_ref, parts):
    total = own_ref[...]
    for part in parts:
        total = total + part[...].astype(F32)
    return total


def activate(own, parts, bias):
    def body(own_ref, bias_ref, *refs):
        parts, (value_ref, slope_ref) = refs[:-2], refs[-2:]
        hidden = add_up(own_ref, parts) + bias_ref[...][:, None, :]
        value, slope = gelu_parts(hidden)
        value_ref[...] = value.astype(BF16)
        slope_ref[...] = slope

    outs = [shape_of(own.shape, BF16), shape_of(own.shape, F32)]
    return call(body, outs, [VM] * (2 + len(parts)), [own, bias, *parts], moved=own.size * 20)


def scale_by_slope(own, parts, slope):
    def body(own_ref, slope_ref, *refs):
        parts, out_ref = refs[:-1], refs[-1]
        out_ref[...] = (add_up(own_ref, parts) * slope_ref[...]).astype(BF16)

    outs = [shape_of(own.shape, BF16)]
    return call(body, outs, [VM] * (2 + len(parts)), [own, slope, *parts], moved=own.size * 16)[0]


def pair_sums(*pairs):
    half, piece, width = pairs[0][0].shape
    count = len(pairs)

    def body(*refs):
        sources, owns, sends = refs[: 2 * count], refs[2 * count : 3 * count], refs[3 * count :]
        for which in range(count):
            keep, came = sources[2 * which : 2 * which + 2]
            owns[which][...] = keep[0] + came[0].astype(F32)
            for entry, send in enumerate(sends, 1):
                send[which] = (keep[entry] + came[entry].astype(F32)).astype(BF16)

    outs = [shape_of((piece, width), F32)] * count + [shape_of((count, piece, width), BF16)] * (half - 1)
    args = [array for pair in pairs for array in pair]
    results = call(body, outs, [VM] * len(args), args, moved=8 * count * half * piece * width)
    return results[:count], results[count:]


def final_sums(owns, parts):
    def body(*refs):
        sources, came, outs = refs[: len(owns)], refs[len(owns) : -len(owns)], refs[-len(owns) :]
        for which, (own, out) in enumerate(zip(sources, outs)):
            total = own[...]
            for part in came:
                total = total + part[which].astype(F32)
            out[...] = total.astype(BF16)

    outs = [shape_of(own.shape, BF16) for own in owns]
    return call(body, outs, [VM] * (len(owns) + len(parts)), [*owns, *parts], moved=8 * sum(own.size for own in owns))


def gather_col(shard, n_col, *before):
    shards = [None] * n_col
    shards[0] = shard
    for mask in range(2, n_col, 2):
        shards[mask] = swap(shard, "col", n_col, mask)
    for mask in range(2, n_col, 2):
        shards[mask] = follow(shards[mask], *before)
    for mask in range(0, n_col, 2):
        shards[mask + 1] = swap(shards[mask], "col", n_col, 1)
    return shards


def gather_row(share, n_row):
    return [share] + [swap(share, "row", n_row, mask) for mask in range(1, n_row)]


def send_row(sends, n_row):
    return [swap(send, "row", n_row, mask) for mask, send in enumerate(sends, 1)]


def local(n_row, n_col, tokens, cotangent, w1_mask, w1_blocks, bias, w2_mask, w2_blocks):
    first_blocks = w1_blocks[0, 0]
    second_blocks = w2_blocks[0, 0]
    model_blocks, hidden_blocks = w1_mask.shape
    first = Slots(w1_mask.shape, first_blocks.shape[0])
    second = Slots(w2_mask.shape, second_blocks.shape[0])
    first_at, second_at = slot_indices([first, second], [w1_mask, w2_mask])
    bias_wide = bias.astype(F32).reshape(hidden_blocks, BLK)

    first_held, first_there = fetch(first_blocks)
    second_held, second_there = fetch(second_blocks)
    shards = gather_col(together(tokens, cotangent), n_col, first_there, second_there)

    hidden_own, hidden_sends, full_tokens = model_to_hidden(
        first, first_at, shards, 0, first_held, True, hidden_blocks, n_row
    )
    hidden_parts = send_row(hidden_sends, n_row)
    act_own, act_sends, full_cotangent = model_to_hidden(
        second, second_at, shards, 1, second_held, False, hidden_blocks, n_row, after=(full_tokens,)
    )
    act_parts = send_row(act_sends, n_row)

    activated, slope = activate(hidden_own, hidden_parts, bias_wide)
    activated_shares = gather_row(activated, n_row)
    grad_hidden = scale_by_slope(act_own, act_parts, slope)
    grad_shares = gather_row(grad_hidden, n_row)

    out_keep, out_send, out_done, w2_grad = hidden_to_model(
        second, second_at, activated_shares, second_held, True, model_blocks, n_col, other=full_cotangent
    )
    out_came = swap(out_send, "col", n_col, 1)
    in_keep, in_send = hidden_to_model(
        first, first_at, grad_shares, first_held, False, model_blocks, n_col, after=(out_done,)
    )
    in_came = swap(in_send, "col", n_col, 1)
    owns, sends = pair_sums((out_keep, out_came), (in_keep, in_came))
    parts = [swap(send, "col", n_col, 2 * entry) for entry, send in enumerate(sends, 1)]
    w1_grad, bias_sum = weight_grad(first, first_at, full_tokens, grad_shares)
    out, tokens_grad = final_sums(owns, parts)
    return (
        out,
        tokens_grad,
        w1_grad[None, None],
        w2_grad[None, None],
        bias_sum.reshape(-1),
    )


def solution(mesh):
    n_row, n_col = mesh.shape["row"], mesh.shape["col"]
    return jax.shard_map(
        lambda *args: local(n_row, n_col, *args),
        mesh=mesh,
        in_specs=(
            P("col", "row"),
            P("col", "row"),
            P("row", "col"),
            P("row", "col", None, None, None),
            P("col"),
            P("col", "row"),
            P("row", "col", None, None, None),
        ),
        out_specs=(
            P("col", "row"),
            P("col", "row"),
            P("row", "col", None, None, None),
            P("row", "col", None, None, None),
            P("col"),
        ),
        check_vma=False,
    )
```

```python
import math

import jax
import jax.numpy as jnp
from jax import lax
from jax.experimental import pallas as pl
from jax.experimental.pallas import tpu as pltpu
from jax.sharding import PartitionSpec as P

BLK = 128
F32 = jnp.float32
BF16 = jnp.bfloat16
VMEM_LIMIT = 12 * 1024 * 1024
VMEM_GRAD = 28 * 1024 * 1024
RING = 24
GRAD_PARTS = (24, 16, 12, 8, 6, 4, 3, 2, 1)

slope_const = math.sqrt(2.0 / math.pi)


def gelu_parts(values):
    inner = slope_const * (values + 0.044715 * values * values * values)
    tangent = jnp.tanh(inner)
    value = 0.5 * values * (1.0 + tangent)
    slope = 0.5 * (1.0 + tangent) + 0.5 * values * (1.0 - tangent * tangent) * slope_const * (
        1.0 + 3.0 * 0.044715 * values * values
    )
    return value, slope


def swap(array, axis, size, mask):
    return lax.ppermute(array, axis, [(place, place ^ mask) for place in range(size)])


def call(body, outs, in_specs, args, scratch=(), grid=None, out_specs=None, flops=0, moved=0, limit=VMEM_LIMIT):
    whole = pl.BlockSpec(memory_space=pltpu.VMEM)
    extra = {} if grid is None else {"grid": grid}
    return pl.pallas_call(
        body,
        out_shape=outs,
        in_specs=in_specs,
        out_specs=[whole] * len(outs) if out_specs is None else out_specs,
        scratch_shapes=list(scratch),
        compiler_params=pltpu.CompilerParams(vmem_limit_bytes=limit),
        cost_estimate=pl.CostEstimate(flops=flops, bytes_accessed=moved, transcendentals=0),
        **extra,
    )(*args)


VM = pl.BlockSpec(memory_space=pltpu.VMEM)
SM = pl.BlockSpec(memory_space=pltpu.SMEM)


def shape_of(shape, dtype):
    return jax.ShapeDtypeStruct(shape, dtype)


def dot(left, right, left_dim, right_dim):
    return lax.dot_general(
        left, right, (((left_dim,), (right_dim,)), ((), ())), preferred_element_type=F32
    )


class Slots:
    def __init__(self, mask_shape, capacity):
        self.rows, self.cols = mask_shape
        self.capacity = capacity
        self.even = self.cols % 8 == 0 and self.cols // 4 <= BLK and capacity == self.rows * (self.cols // 4)
        self.group = self.cols // 4 if self.even else 1
        self.groups = capacity // self.group
        self.spare = 0 if self.even else 1

    def uneven_slots(self, mask):
        self.even, self.group, self.groups, self.spare = False, 1, self.capacity, 1
        flat = mask.reshape(-1)
        count = flat.shape[0]
        places = jnp.arange(count, dtype=jnp.int32)
        lane = jnp.arange(self.cols, dtype=jnp.int32)
        within = jnp.sum(jnp.where(lane[None, :] <= lane[:, None], mask[:, None, :], 0), axis=2)
        row_sum = jnp.sum(mask, axis=1)
        line = jnp.arange(self.rows, dtype=jnp.int32)
        before = jnp.sum(jnp.where(line[None, :] < line[:, None], row_sum[None, :], 0), axis=1)
        rank = (within + before[:, None] - 1).reshape(-1)
        slot = jnp.arange(self.capacity, dtype=jnp.int32)
        hit = (rank[None, :] == slot[:, None]) & (flat[None, :] > 0)
        order = jnp.sum(jnp.where(hit, places[None, :], 0), axis=1)
        live = slot < jnp.sum(flat)
        row = jnp.where(live, order // self.cols, self.rows)
        col = jnp.where(live, order % self.cols, self.cols)
        return row, col


def index_kernel(layout, mask, out_ref):
    rows, cols, group = layout.rows, layout.cols, layout.group
    lower = lax.broadcasted_iota(jnp.int32, (cols, cols), 0)
    upper = lax.broadcasted_iota(jnp.int32, (cols, cols), 1)
    ramp = jnp.where(lower <= upper, 1.0, 0.0).astype(BF16)
    rank = dot(mask.astype(BF16), ramp, 1, 0)
    place = lax.broadcasted_iota(jnp.int32, (rows, cols), 1).astype(F32)
    lane = lax.broadcasted_iota(jnp.int32, (rows, BLK), 1)
    found = jnp.zeros((rows, BLK), F32)
    for slot in range(group):
        hit = (rank == float(slot + 1)) & (mask > 0.0)
        column = jnp.sum(jnp.where(hit, place, 0.0), axis=1, keepdims=True)
        found = jnp.where(lane == slot, column, found)
    out_ref[...] = found.astype(jnp.int32)


def slot_indices(layouts, masks):
    if not all(layout.even for layout in layouts):
        return [layout.uneven_slots(mask) for layout, mask in zip(layouts, masks)]
    turned = [layout.rows > layout.cols for layout in layouts]
    arrays = [mask.T if turn else mask for mask, turn in zip(masks, turned)]

    def body(*refs):
        for which, (layout, turn) in enumerate(zip(layouts, turned)):
            mask = refs[which][...].astype(F32)
            index_kernel(layout, mask.T if turn else mask, refs[len(layouts) + which])

    outs = call(
        body,
        [shape_of((layout.rows, BLK), jnp.int32) for layout in layouts],
        [pl.BlockSpec(array.shape, lambda step: (0, 0)) for array in arrays],
        [pltpu.with_memory_space_constraint(array, pltpu.HBM) for array in arrays],
        grid=(1,),
    )
    return [(out, out) for out in outs]


def read_slot(layout, row_ref, col_ref, group, member):
    if layout.even:
        return group, col_ref[group, member]
    return row_ref[group], col_ref[group]


def add_forward(layout, row_ref, col_ref, first, here, source, blocks, total):
    group = layout.group
    for near in range(here):
        if layout.even:
            left = source[first + near]
            width = 2 if group % 2 == 0 else 1
            for member in range(0, group, width):
                place = near * group + member
                right = [blocks[place + more] for more in range(width)]
                right = right[0] if width == 1 else jnp.concatenate(right, axis=1)
                product = dot(left, right, 1, 0)
                for more in range(width):
                    col = col_ref[first + near, member + more]
                    total[col] += product[:, more * BLK : (more + 1) * BLK]
        else:
            row, col = read_slot(layout, row_ref, col_ref, first + near, 0)
            total[col] += dot(source[row], blocks[near], 1, 0)


def add_backward(layout, row_ref, col_ref, first, here, source, blocks, total):
    group = layout.group
    for near in range(here):
        if layout.even:
            width = 2 if group % 2 == 0 else 1
            result = None
            for member in range(0, group, width):
                place = near * group + member
                cols = [col_ref[first + near, member + more] for more in range(width)]
                left = [source[col] for col in cols]
                right = [blocks[place + more] for more in range(width)]
                left = left[0] if width == 1 else jnp.concatenate(left, axis=1)
                right = right[0] if width == 1 else jnp.concatenate(right, axis=1)
                product = dot(left, right, 1, 1)
                result = product if result is None else result + product
            total[first + near] = result
        else:
            row, col = read_slot(layout, row_ref, col_ref, first + near, 0)
            total[row] += dot(source[col], blocks[near], 1, 1)


def block_products(layout, row_ref, col_ref, first, here, left, right, out):
    group = layout.group
    for near in range(here):
        if layout.even:
            turned = left[first + near].T
            width = 2 if group % 2 == 0 else 1
            for member in range(0, group, width):
                place = near * group + member
                cols = [col_ref[first + near, member + more] for more in range(width)]
                wide = [right[col] for col in cols]
                wide = wide[0] if width == 1 else jnp.concatenate(wide, axis=1)
                product = dot(turned, wide, 1, 0)
                for more in range(width):
                    out[place + more] = product[:, more * BLK : (more + 1) * BLK]
        else:
            row, col = read_slot(layout, row_ref, col_ref, first + near, 0)
            live = row < layout.rows
            product = dot(left[row].T, right[col], 1, 0)
            out[near] = jnp.where(live, product, 0.0)


def gather_model(me, shards, which, stage, full):
    piece = shards[0].shape[1]
    for mask, shard in enumerate(shards):
        start = pl.multiple_of((me ^ mask) * piece, piece)
        stage[pl.ds(start, piece), :] = shard[which].astype(F32)
    for block in range(shards[0].shape[2] // BLK):
        full[block] = stage[:, block * BLK : (block + 1) * BLK].astype(full.dtype)


def gather_hidden(me, shares, full):
    blocks, piece, _ = shares[0].shape
    for mask, share in enumerate(shares):
        start = pl.multiple_of((me ^ mask) * piece, piece)
        full[pl.ds(0, blocks), pl.ds(start, piece), :] = share[...]


def parts_of(layout, choices):
    parts = next(parts for parts in choices if layout.groups % parts == 0)
    return parts, layout.groups // parts, layout.capacity // parts


def apply_cost(layout, tokens):
    return 2 * layout.capacity * BLK * BLK * tokens, 2 * layout.capacity * BLK * BLK


def together(first, second):
    def body(first_ref, second_ref, out_ref):
        out_ref[0] = first_ref[...]
        out_ref[1] = second_ref[...]

    block = pl.BlockSpec(first.shape, lambda step: (0, 0))
    return call(
        body,
        [shape_of((2, *first.shape), first.dtype)],
        [block, block],
        [pltpu.with_memory_space_constraint(array, pltpu.HBM) for array in (first, second)],
        grid=(1,),
        moved=8 * first.size,
    )[0]


def fetch(blocks):
    def body(from_ref, to_ref, token, done):
        copy = pltpu.make_async_copy(from_ref, to_ref, done)
        copy.start()
        token[...] = jnp.zeros_like(token)
        copy.wait()

    return call(
        body,
        [pltpu.VMEM(blocks.shape, blocks.dtype), shape_of((8, BLK), F32)],
        [pl.BlockSpec(memory_space=pltpu.HBM)],
        [pltpu.with_memory_space_constraint(blocks, pltpu.HBM)],
        scratch=[pltpu.SemaphoreType.DMA],
        moved=4 * blocks.size,
    )


def follow(array, *before):
    def body(array_ref, *refs):
        refs[-1][...] = array_ref[...]

    specs = [VM] * (1 + len(before))
    return call(body, [shape_of(array.shape, array.dtype)], specs, [array, *before], moved=4 * array.size)[0]


def model_to_hidden(layout, rows_cols, shards, which, blocks, forward, hidden_blocks, n_row, after=()):
    count = len(shards)
    _, part, width = shards[0].shape
    tokens = part * count
    model_blocks = width // BLK
    piece = tokens // n_row
    spare = layout.spare

    def body(row_ref, col_ref, *refs):
        shard_refs = refs[:count]
        weights, own, *sends, whole, stage, full, total = refs[count + len(after) :]
        gather_model(lax.axis_index("col"), shard_refs, which, stage, full)
        if spare:
            full[model_blocks] = jnp.zeros((tokens, BLK), BF16)
        if forward or spare:
            total[...] = jnp.zeros_like(total)
        work = add_forward if forward else add_backward
        work(layout, row_ref, col_ref, 0, layout.groups, full, weights, total)
        me = lax.axis_index("row")
        for mask, out in enumerate([own] + sends):
            start = pl.multiple_of((me ^ mask) * piece, piece)
            out[...] = total[pl.ds(0, hidden_blocks), pl.ds(start, piece), :].astype(out.dtype)
        whole[...] = full[pl.ds(0, model_blocks)]

    share = (hidden_blocks, piece, BLK)
    outs = [shape_of(share, F32)] + [shape_of(share, BF16)] * (n_row - 1)
    outs += [shape_of((model_blocks, tokens, BLK), BF16)]
    flops, moved = apply_cost(layout, tokens)
    args = [*rows_cols, *shards, *after, pltpu.with_memory_space_constraint(blocks, pltpu.VMEM)]
    own, *sends, whole = call(
        body,
        outs,
        [SM, SM] + [VM] * (len(args) - 2),
        args,
        scratch=[
            pltpu.VMEM((tokens, width), F32),
            pltpu.VMEM((model_blocks + spare, tokens, BLK), BF16),
            pltpu.VMEM((hidden_blocks + spare, tokens, BLK), F32),
        ],
        flops=flops,
        moved=moved,
    )
    return own, sends, whole


def hidden_to_model(layout, rows_cols, shares, blocks, forward, model_blocks, n_col, other=None, after=()):
    count = len(shares)
    hidden_blocks, part, _ = shares[0].shape
    tokens = part * count
    piece = tokens // n_col
    half = n_col // 2
    spare = layout.spare
    grads = other is not None

    def body(row_ref, col_ref, *refs):
        share_refs, refs = refs[:count], refs[count + len(after) :]
        if grads:
            other_ref, weights, keep, send, token, grad, full, total, other_full, made, done = refs
            token[...] = jnp.zeros_like(token)
        else:
            weights, keep, send, full, total = refs
        gather_hidden(lax.axis_index("row"), share_refs, full)
        if spare:
            full[hidden_blocks] = jnp.zeros((tokens, BLK), BF16)
        if forward or spare:
            total[...] = jnp.zeros_like(total)
        if grads:
            if spare:
                other_full[pl.ds(0, model_blocks)] = other_ref[...]
                other_full[model_blocks] = jnp.zeros((tokens, BLK), BF16)
                other_ref = other_full
            copies = send_products(layout, row_ref, col_ref, full, other_ref, made, grad, done)
        work = add_forward if forward else add_backward
        work(layout, row_ref, col_ref, 0, layout.groups, full, weights, total)
        me = lax.axis_index("col")
        for entry in range(half):
            mine = pl.multiple_of((me ^ (2 * entry)) * piece, piece)
            theirs = pl.multiple_of((me ^ (2 * entry + 1)) * piece, piece)
            for block in range(model_blocks):
                lanes = pl.ds(block * BLK, BLK)
                keep[entry, :, lanes] = total[block, pl.ds(mine, piece), :]
                send[entry, :, lanes] = total[block, pl.ds(theirs, piece), :].astype(BF16)
        if grads:
            for copy in copies:
                copy.wait()

    pair = (half, piece, model_blocks * BLK)
    outs = [shape_of(pair, F32), shape_of(pair, BF16)]
    out_specs = [VM] * (4 if grads else 2)
    args = [*rows_cols, *shares, *after]
    scratch = [
        pltpu.VMEM((hidden_blocks + spare, tokens, BLK), BF16),
        pltpu.VMEM((model_blocks + spare, tokens, BLK), F32),
    ]
    flops, moved = apply_cost(layout, tokens)
    if grads:
        outs += [shape_of((8, BLK), F32), shape_of((layout.capacity, BLK, BLK), F32)]
        out_specs[3] = pl.BlockSpec(memory_space=pltpu.HBM)
        args += [other]
        scratch += [
            pltpu.VMEM((model_blocks + spare, tokens, BLK), BF16),
            *ring_scratch(layout),
        ]
        flops, moved = 2 * flops, 3 * moved
    args += [pltpu.with_memory_space_constraint(blocks, pltpu.VMEM)]
    return call(
        body,
        outs,
        [SM, SM] + [VM] * (len(args) - 2),
        args,
        scratch=scratch,
        out_specs=out_specs,
        flops=flops,
        moved=moved,
        limit=VMEM_GRAD if grads else VMEM_LIMIT,
    )


def ring_scratch(layout):
    parts, _, size = parts_of(layout, GRAD_PARTS)
    slots = min(RING, parts)
    return [pltpu.VMEM((slots, size, BLK, BLK), F32), pltpu.SemaphoreType.DMA((slots,))]


def send_products(layout, row_ref, col_ref, left, right, ring, grad, done):
    parts, here, size = parts_of(layout, GRAD_PARTS)
    slots = ring.shape[0]
    copies = []
    for part in range(parts):
        slot = part % slots
        if part >= slots:
            copies[part - slots].wait()
        block_products(layout, row_ref, col_ref, part * here, here, left, right, ring.at[slot])
        place = pl.ds(part * size, size)
        copies.append(pltpu.make_async_copy(ring.at[slot], grad.at[place], done.at[slot]))
        copies[-1].start()
    return copies[-slots:]


def weight_grad(layout, rows_cols, left, shares):
    spare = layout.spare
    count = len(shares)
    left_blocks, tokens, _ = left.shape
    hidden_blocks = shares[0].shape[0]

    def body(row_ref, col_ref, left_ref, *refs):
        share_refs, (grad, sum_ref, made, done, full, *wide) = refs[:count], refs[count:]
        gather_hidden(lax.axis_index("row"), share_refs, full)
        if spare:
            full[hidden_blocks] = jnp.zeros((tokens, BLK), BF16)
            wide[0][pl.ds(0, left_blocks)] = left_ref[...]
            wide[0][left_blocks] = jnp.zeros((tokens, BLK), BF16)
            left_ref = wide[0]
        copies = send_products(layout, row_ref, col_ref, left_ref, full, made, grad, done)
        for block in range(hidden_blocks):
            sum_ref[pl.ds(block, 1), :] = jnp.sum(full[block].astype(F32), axis=0, keepdims=True)
        for copy in copies:
            copy.wait()

    flops, moved = apply_cost(layout, tokens)
    out = shape_of((layout.capacity, BLK, BLK), F32)
    scratch = ring_scratch(layout)
    scratch += [pltpu.VMEM((hidden_blocks + spare, tokens, BLK), BF16)]
    if spare:
        scratch += [pltpu.VMEM((left_blocks + 1, tokens, BLK), BF16)]
    return call(
        body,
        [out, shape_of((hidden_blocks, BLK), F32)],
        [SM, SM, VM] + [VM] * count,
        [*rows_cols, left, *shares],
        scratch=scratch,
        out_specs=[pl.BlockSpec(memory_space=pltpu.HBM), VM],
        flops=flops,
        moved=2 * moved,
        limit=VMEM_GRAD,
    )


def add_up(own_ref, parts):
    total = own_ref[...]
    for part in parts:
        total = total + part[...].astype(F32)
    return total


def activate(own, parts, bias):
    def body(own_ref, bias_ref, *refs):
        parts, (value_ref, slope_ref) = refs[:-2], refs[-2:]
        hidden = add_up(own_ref, parts) + bias_ref[...][:, None, :]
        value, slope = gelu_parts(hidden)
        value_ref[...] = value.astype(BF16)
        slope_ref[...] = slope

    outs = [shape_of(own.shape, BF16), shape_of(own.shape, F32)]
    return call(body, outs, [VM] * (2 + len(parts)), [own, bias, *parts], moved=own.size * 20)


def scale_by_slope(own, parts, slope):
    def body(own_ref, slope_ref, *refs):
        parts, (out_ref, token) = refs[:-2], refs[-2:]
        out_ref[...] = (add_up(own_ref, parts) * slope_ref[...]).astype(BF16)
        token[...] = jnp.zeros_like(token)

    outs = [shape_of(own.shape, BF16), shape_of((8, BLK), F32)]
    return call(body, outs, [VM] * (2 + len(parts)), [own, slope, *parts], moved=own.size * 16)


def pair_sums(*pairs):
    half, piece, width = pairs[0][0].shape
    count = len(pairs)

    def body(*refs):
        sources, owns, sends = refs[: 2 * count], refs[2 * count : 3 * count], refs[3 * count :]
        for which in range(count):
            keep, came = sources[2 * which : 2 * which + 2]
            owns[which][...] = keep[0] + came[0].astype(F32)
            for entry, send in enumerate(sends, 1):
                send[which] = (keep[entry] + came[entry].astype(F32)).astype(BF16)

    outs = [shape_of((piece, width), F32)] * count + [shape_of((count, piece, width), BF16)] * (half - 1)
    args = [array for pair in pairs for array in pair]
    results = call(body, outs, [VM] * len(args), args, moved=8 * count * half * piece * width)
    return results[:count], results[count:]


def final_sums(owns, parts):
    def body(*refs):
        sources, came, outs = refs[: len(owns)], refs[len(owns) : -len(owns)], refs[-len(owns) :]
        for which, (own, out) in enumerate(zip(sources, outs)):
            total = own[...]
            for part in came:
                total = total + part[which].astype(F32)
            out[...] = total.astype(BF16)

    outs = [shape_of(own.shape, BF16) for own in owns]
    return call(body, outs, [VM] * (len(owns) + len(parts)), [*owns, *parts], moved=8 * sum(own.size for own in owns))


def gather_col(shard, n_col, *before):
    shards = [None] * n_col
    shards[0] = shard
    for mask in range(2, n_col, 2):
        shards[mask] = swap(shard, "col", n_col, mask)
    for mask in range(2, n_col, 2):
        shards[mask] = follow(shards[mask], *before)
    for mask in range(0, n_col, 2):
        shards[mask + 1] = swap(shards[mask], "col", n_col, 1)
    return shards


def gather_row(share, n_row):
    return [share] + [swap(share, "row", n_row, mask) for mask in range(1, n_row)]


def send_row(sends, n_row):
    return [swap(send, "row", n_row, mask) for mask, send in enumerate(sends, 1)]


def local(n_row, n_col, tokens, cotangent, w1_mask, w1_blocks, bias, w2_mask, w2_blocks):
    first_blocks = w1_blocks[0, 0]
    second_blocks = w2_blocks[0, 0]
    model_blocks, hidden_blocks = w1_mask.shape
    first = Slots(w1_mask.shape, first_blocks.shape[0])
    second = Slots(w2_mask.shape, second_blocks.shape[0])
    first_at, second_at = slot_indices([first, second], [w1_mask, w2_mask])
    bias_wide = bias.astype(F32).reshape(hidden_blocks, BLK)

    first_held, first_there = fetch(first_blocks)
    second_held, second_there = fetch(second_blocks)
    shards = gather_col(together(tokens, cotangent), n_col, first_there, second_there)

    hidden_own, hidden_sends, full_tokens = model_to_hidden(
        first, first_at, shards, 0, first_held, True, hidden_blocks, n_row
    )
    hidden_parts = send_row(hidden_sends, n_row)
    act_own, act_sends, full_cotangent = model_to_hidden(
        second, second_at, shards, 1, second_held, False, hidden_blocks, n_row, after=(full_tokens,)
    )
    act_parts = send_row(act_sends, n_row)

    activated, slope = activate(hidden_own, hidden_parts, bias_wide)
    activated_shares = gather_row(activated, n_row)
    grad_hidden, grad_there = scale_by_slope(act_own, act_parts, slope)
    met = swap(grad_there, "col", n_col, 1)
    grad_later = follow(grad_hidden, met)
    grad_shares = [grad_hidden]
    for mask in range(1, n_row):
        grad_shares += [swap(grad_hidden if mask == n_row - 1 else grad_later, "row", n_row, mask)]

    out_keep, out_send, out_done, w2_grad = hidden_to_model(
        second, second_at, activated_shares, second_held, True, model_blocks, n_col, other=full_cotangent
    )
    out_came = swap(out_send, "col", n_col, 1)
    in_keep, in_send = hidden_to_model(
        first, first_at, grad_shares, first_held, False, model_blocks, n_col, after=(out_done,)
    )
    in_came = swap(in_send, "col", n_col, 1)
    owns, sends = pair_sums((out_keep, out_came), (in_keep, in_came))
    parts = [swap(send, "col", n_col, 2 * entry) for entry, send in enumerate(sends, 1)]
    w1_grad, bias_sum = weight_grad(first, first_at, full_tokens, grad_shares)
    out, tokens_grad = final_sums(owns, parts)
    return (
        out,
        tokens_grad,
        w1_grad[None, None],
        w2_grad[None, None],
        bias_sum.reshape(-1),
    )


def solution(mesh):
    n_row, n_col = mesh.shape["row"], mesh.shape["col"]
    return jax.shard_map(
        lambda *args: local(n_row, n_col, *args),
        mesh=mesh,
        in_specs=(
            P("col", "row"),
            P("col", "row"),
            P("row", "col"),
            P("row", "col", None, None, None),
            P("col"),
            P("col", "row"),
            P("row", "col", None, None, None),
        ),
        out_specs=(
            P("col", "row"),
            P("col", "row"),
            P("row", "col", None, None, None),
            P("row", "col", None, None, None),
            P("col"),
        ),
        check_vma=False,
    )
```

```python
import functools
import math

import jax
import jax.numpy as jnp
from jax import lax
from jax.experimental import pallas as pl
from jax.experimental.pallas import tpu as pltpu
from jax.sharding import PartitionSpec as P

BLK = 128
F32 = jnp.float32
BF16 = jnp.bfloat16
VMEM_LIMIT = 12 * 1024 * 1024
VMEM_GRAD = 28 * 1024 * 1024
RING = 24
GRAD_PARTS = (24, 16, 12, 8, 6, 4, 3, 2, 1)

slope_const = math.sqrt(2.0 / math.pi)


def gelu_parts(values):
    inner = slope_const * (values + 0.044715 * values * values * values)
    tangent = jnp.tanh(inner)
    value = 0.5 * values * (1.0 + tangent)
    slope = 0.5 * (1.0 + tangent) + 0.5 * values * (1.0 - tangent * tangent) * slope_const * (
        1.0 + 3.0 * 0.044715 * values * values
    )
    return value, slope


def swap(array, axis, size, mask):
    return lax.ppermute(array, axis, [(place, place ^ mask) for place in range(size)])


def call(body, outs, in_specs, args, scratch=(), grid=None, out_specs=None, flops=0, moved=0, limit=VMEM_LIMIT):
    whole = pl.BlockSpec(memory_space=pltpu.VMEM)
    extra = {} if grid is None else {"grid": grid}
    return pl.pallas_call(
        body,
        out_shape=outs,
        in_specs=in_specs,
        out_specs=[whole] * len(outs) if out_specs is None else out_specs,
        scratch_shapes=list(scratch),
        compiler_params=pltpu.CompilerParams(vmem_limit_bytes=limit),
        cost_estimate=pl.CostEstimate(flops=flops, bytes_accessed=moved, transcendentals=0),
        **extra,
    )(*args)


VM = pl.BlockSpec(memory_space=pltpu.VMEM)
SM = pl.BlockSpec(memory_space=pltpu.SMEM)


def shape_of(shape, dtype):
    return jax.ShapeDtypeStruct(shape, dtype)


def dot(left, right, left_dim, right_dim):
    return lax.dot_general(
        left, right, (((left_dim,), (right_dim,)), ((), ())), preferred_element_type=F32
    )


class Slots:
    def __init__(self, mask_shape, capacity):
        self.rows, self.cols = mask_shape
        self.capacity = capacity
        self.even = self.cols % 8 == 0 and self.cols // 4 <= BLK and capacity == self.rows * (self.cols // 4)
        self.group = self.cols // 4 if self.even else 1
        self.groups = capacity // self.group
        self.spare = 0 if self.even else 1

    def uneven_slots(self, mask):
        self.even, self.group, self.groups, self.spare = False, 1, self.capacity, 1
        flat = mask.reshape(-1)
        count = flat.shape[0]
        places = jnp.arange(count, dtype=jnp.int32)
        lane = jnp.arange(self.cols, dtype=jnp.int32)
        within = jnp.sum(jnp.where(lane[None, :] <= lane[:, None], mask[:, None, :], 0), axis=2)
        row_sum = jnp.sum(mask, axis=1)
        line = jnp.arange(self.rows, dtype=jnp.int32)
        before = jnp.sum(jnp.where(line[None, :] < line[:, None], row_sum[None, :], 0), axis=1)
        rank = (within + before[:, None] - 1).reshape(-1)
        slot = jnp.arange(self.capacity, dtype=jnp.int32)
        hit = (rank[None, :] == slot[:, None]) & (flat[None, :] > 0)
        order = jnp.sum(jnp.where(hit, places[None, :], 0), axis=1)
        live = slot < jnp.sum(flat)
        row = jnp.where(live, order // self.cols, self.rows)
        col = jnp.where(live, order % self.cols, self.cols)
        return row, col


def index_kernel(layout, mask, out_ref):
    rows, cols, group = layout.rows, layout.cols, layout.group
    lower = lax.broadcasted_iota(jnp.int32, (cols, cols), 0)
    upper = lax.broadcasted_iota(jnp.int32, (cols, cols), 1)
    ramp = jnp.where(lower <= upper, 1.0, 0.0).astype(BF16)
    rank = dot(mask.astype(BF16), ramp, 1, 0)
    place = lax.broadcasted_iota(jnp.int32, (rows, cols), 1).astype(F32)
    lane = lax.broadcasted_iota(jnp.int32, (rows, BLK), 1)
    found = jnp.zeros((rows, BLK), F32)
    for slot in range(group):
        hit = (rank == float(slot + 1)) & (mask > 0.0)
        column = jnp.sum(jnp.where(hit, place, 0.0), axis=1, keepdims=True)
        found = jnp.where(lane == slot, column, found)
    out_ref[...] = found.astype(jnp.int32)


def slot_indices(layouts, masks):
    if not all(layout.even for layout in layouts):
        return [layout.uneven_slots(mask) for layout, mask in zip(layouts, masks)]
    turned = [layout.rows > layout.cols for layout in layouts]
    arrays = [mask.T if turn else mask for mask, turn in zip(masks, turned)]

    def body(*refs):
        for which, (layout, turn) in enumerate(zip(layouts, turned)):
            mask = refs[which][...].astype(F32)
            index_kernel(layout, mask.T if turn else mask, refs[len(layouts) + which])

    outs = call(
        body,
        [shape_of((layout.rows, BLK), jnp.int32) for layout in layouts],
        [pl.BlockSpec(array.shape, lambda step: (0, 0)) for array in arrays],
        [pltpu.with_memory_space_constraint(array, pltpu.HBM) for array in arrays],
        grid=(1,),
    )
    return [(out, out) for out in outs]


def read_slot(layout, row_ref, col_ref, group, member):
    if layout.even:
        return group, col_ref[group, member]
    return row_ref[group], col_ref[group]


def add_forward(layout, row_ref, col_ref, first, here, source, blocks, total):
    group = layout.group
    for near in range(here):
        if layout.even:
            left = source[first + near]
            width = 2 if group % 2 == 0 else 1
            for member in range(0, group, width):
                place = near * group + member
                right = [blocks[place + more] for more in range(width)]
                right = right[0] if width == 1 else jnp.concatenate(right, axis=1)
                product = dot(left, right, 1, 0)
                for more in range(width):
                    col = col_ref[first + near, member + more]
                    total[col] += product[:, more * BLK : (more + 1) * BLK]
        else:
            row, col = read_slot(layout, row_ref, col_ref, first + near, 0)
            total[col] += dot(source[row], blocks[near], 1, 0)


def add_backward(layout, row_ref, col_ref, first, here, source, blocks, total, turned=False):
    group = layout.group
    side = 0 if turned else 1
    for near in range(here):
        if layout.even:
            width = 2 if group % 2 == 0 else 1
            result = None
            for member in range(0, group, width):
                place = near * group + member
                cols = [col_ref[first + near, member + more] for more in range(width)]
                left = [source[col] for col in cols]
                right = [blocks[place + more] for more in range(width)]
                left = left[0] if width == 1 else jnp.concatenate(left, axis=1)
                right = right[0] if width == 1 else jnp.concatenate(right, axis=side)
                product = dot(left, right, 1, side)
                result = product if result is None else result + product
            total[first + near] = result
        else:
            row, col = read_slot(layout, row_ref, col_ref, first + near, 0)
            total[row] += dot(source[col], blocks[near], 1, side)


def block_products(layout, row_ref, col_ref, first, here, left, right, out):
    group = layout.group
    for near in range(here):
        if layout.even:
            turned = left[first + near].T
            width = 2 if group % 2 == 0 else 1
            for member in range(0, group, width):
                place = near * group + member
                cols = [col_ref[first + near, member + more] for more in range(width)]
                wide = [right[col] for col in cols]
                wide = wide[0] if width == 1 else jnp.concatenate(wide, axis=1)
                product = dot(turned, wide, 1, 0)
                for more in range(width):
                    out[place + more] = product[:, more * BLK : (more + 1) * BLK]
        else:
            row, col = read_slot(layout, row_ref, col_ref, first + near, 0)
            live = row < layout.rows
            product = dot(left[row].T, right[col], 1, 0)
            out[near] = jnp.where(live, product, 0.0)


def gather_model(me, shards, which, stage, full):
    piece = shards[0].shape[1]
    for mask, shard in enumerate(shards):
        start = pl.multiple_of((me ^ mask) * piece, piece)
        stage[pl.ds(start, piece), :] = shard[which].astype(F32)
    for block in range(shards[0].shape[2] // BLK):
        full[block] = stage[:, block * BLK : (block + 1) * BLK].astype(full.dtype)


def gather_hidden(me, shares, full):
    blocks, piece, _ = shares[0].shape
    for mask, share in enumerate(shares):
        start = pl.multiple_of((me ^ mask) * piece, piece)
        full[pl.ds(0, blocks), pl.ds(start, piece), :] = share[...]


def parts_of(layout, choices):
    parts = next(parts for parts in choices if layout.groups % parts == 0)
    return parts, layout.groups // parts, layout.capacity // parts


def apply_cost(layout, tokens):
    return 2 * layout.capacity * BLK * BLK * tokens, 2 * layout.capacity * BLK * BLK


def together(first, second):
    def body(first_ref, second_ref, out_ref):
        out_ref[0] = first_ref[...]
        out_ref[1] = second_ref[...]

    block = pl.BlockSpec(first.shape, lambda step: (0, 0))
    return call(
        body,
        [shape_of((2, *first.shape), first.dtype)],
        [block, block],
        [pltpu.with_memory_space_constraint(array, pltpu.HBM) for array in (first, second)],
        grid=(1,),
        moved=8 * first.size,
    )[0]


def fetch(blocks):
    def body(from_ref, to_ref, token, done):
        copy = pltpu.make_async_copy(from_ref, to_ref, done)
        copy.start()
        token[...] = jnp.zeros_like(token)
        copy.wait()

    return call(
        body,
        [pltpu.VMEM(blocks.shape, blocks.dtype), shape_of((8, BLK), F32)],
        [pl.BlockSpec(memory_space=pltpu.HBM)],
        [pltpu.with_memory_space_constraint(blocks, pltpu.HBM)],
        scratch=[pltpu.SemaphoreType.DMA],
        moved=4 * blocks.size,
    )


def follow(array, *before):
    def body(array_ref, *refs):
        refs[-1][...] = array_ref[...]

    specs = [VM] * (1 + len(before))
    return call(body, [shape_of(array.shape, array.dtype)], specs, [array, *before], moved=4 * array.size)[0]


def turn(blocks, after):
    count = blocks.shape[0]

    def body(from_ref, after_ref, to_ref, token):
        token[...] = jnp.zeros_like(token)

        def one(place, carry):
            to_ref[place] = from_ref[place].T
            return carry

        lax.fori_loop(0, count, one, 0, unroll=math.gcd(count, 48))

    return call(
        body,
        [pltpu.VMEM(blocks.shape, blocks.dtype), shape_of((8, BLK), F32)],
        [VM, VM],
        [pltpu.with_memory_space_constraint(blocks, pltpu.VMEM), after],
        moved=2 * blocks.size,
    )


def model_to_hidden(layout, rows_cols, shards, which, blocks, forward, hidden_blocks, n_row, after=()):
    count = len(shards)
    _, part, width = shards[0].shape
    tokens = part * count
    model_blocks = width // BLK
    piece = tokens // n_row
    spare = layout.spare

    def body(row_ref, col_ref, *refs):
        shard_refs = refs[:count]
        weights, own, *sends, whole, stage, full, total = refs[count + len(after) :]
        gather_model(lax.axis_index("col"), shard_refs, which, stage, full)
        if spare:
            full[model_blocks] = jnp.zeros((tokens, BLK), BF16)
        if forward or spare:
            total[...] = jnp.zeros_like(total)
        work = add_forward if forward else add_backward
        work(layout, row_ref, col_ref, 0, layout.groups, full, weights, total)
        me = lax.axis_index("row")
        for mask, out in enumerate([own] + sends):
            start = pl.multiple_of((me ^ mask) * piece, piece)
            out[...] = total[pl.ds(0, hidden_blocks), pl.ds(start, piece), :].astype(out.dtype)
        whole[...] = full[pl.ds(0, model_blocks)]

    share = (hidden_blocks, piece, BLK)
    outs = [shape_of(share, F32)] + [shape_of(share, BF16)] * (n_row - 1)
    outs += [shape_of((model_blocks, tokens, BLK), BF16)]
    flops, moved = apply_cost(layout, tokens)
    args = [*rows_cols, *shards, *after, pltpu.with_memory_space_constraint(blocks, pltpu.VMEM)]
    own, *sends, whole = call(
        body,
        outs,
        [SM, SM] + [VM] * (len(args) - 2),
        args,
        scratch=[
            pltpu.VMEM((tokens, width), F32),
            pltpu.VMEM((model_blocks + spare, tokens, BLK), BF16),
            pltpu.VMEM((hidden_blocks + spare, tokens, BLK), F32),
        ],
        flops=flops,
        moved=moved,
    )
    return own, sends, whole


def hidden_to_model(layout, rows_cols, shares, blocks, forward, model_blocks, n_col, other=None, after=()):
    count = len(shares)
    hidden_blocks, part, _ = shares[0].shape
    tokens = part * count
    piece = tokens // n_col
    half = n_col // 2
    spare = layout.spare
    grads = other is not None

    def body(row_ref, col_ref, *refs):
        share_refs, refs = refs[:count], refs[count + len(after) :]
        if grads:
            other_ref, weights, keep, send, token, grad, full, total, other_full, made, done = refs
            token[...] = jnp.zeros_like(token)
        else:
            weights, keep, send, full, total = refs
        gather_hidden(lax.axis_index("row"), share_refs, full)
        if spare:
            full[hidden_blocks] = jnp.zeros((tokens, BLK), BF16)
        if forward or spare:
            total[...] = jnp.zeros_like(total)
        if grads:
            if spare:
                other_full[pl.ds(0, model_blocks)] = other_ref[...]
                other_full[model_blocks] = jnp.zeros((tokens, BLK), BF16)
                other_ref = other_full
            copies = send_products(layout, row_ref, col_ref, full, other_ref, made, grad, done)
        work = add_forward if forward else functools.partial(add_backward, turned=True)
        work(layout, row_ref, col_ref, 0, layout.groups, full, weights, total)
        me = lax.axis_index("col")
        for entry in range(half):
            mine = pl.multiple_of((me ^ (2 * entry)) * piece, piece)
            theirs = pl.multiple_of((me ^ (2 * entry + 1)) * piece, piece)
            for block in range(model_blocks):
                lanes = pl.ds(block * BLK, BLK)
                keep[entry, :, lanes] = total[block, pl.ds(mine, piece), :]
                send[entry, :, lanes] = total[block, pl.ds(theirs, piece), :].astype(BF16)
        if grads:
            for copy in copies:
                copy.wait()

    pair = (half, piece, model_blocks * BLK)
    outs = [shape_of(pair, F32), shape_of(pair, BF16)]
    out_specs = [VM] * (4 if grads else 2)
    args = [*rows_cols, *shares, *after]
    scratch = [
        pltpu.VMEM((hidden_blocks + spare, tokens, BLK), BF16),
        pltpu.VMEM((model_blocks + spare, tokens, BLK), F32),
    ]
    flops, moved = apply_cost(layout, tokens)
    if grads:
        outs += [shape_of((8, BLK), F32), shape_of((layout.capacity, BLK, BLK), F32)]
        out_specs[3] = pl.BlockSpec(memory_space=pltpu.HBM)
        args += [other]
        scratch += [
            pltpu.VMEM((model_blocks + spare, tokens, BLK), BF16),
            *ring_scratch(layout),
        ]
        flops, moved = 2 * flops, 3 * moved
    args += [pltpu.with_memory_space_constraint(blocks, pltpu.VMEM)]
    return call(
        body,
        outs,
        [SM, SM] + [VM] * (len(args) - 2),
        args,
        scratch=scratch,
        out_specs=out_specs,
        flops=flops,
        moved=moved,
        limit=VMEM_GRAD if grads else VMEM_LIMIT,
    )


def ring_scratch(layout):
    parts, _, size = parts_of(layout, GRAD_PARTS)
    slots = min(RING, parts)
    return [pltpu.VMEM((slots, size, BLK, BLK), F32), pltpu.SemaphoreType.DMA((slots,))]


def send_products(layout, row_ref, col_ref, left, right, ring, grad, done):
    parts, here, size = parts_of(layout, GRAD_PARTS)
    slots = ring.shape[0]
    copies = []
    for part in range(parts):
        slot = part % slots
        if part >= slots:
            copies[part - slots].wait()
        block_products(layout, row_ref, col_ref, part * here, here, left, right, ring.at[slot])
        place = pl.ds(part * size, size)
        copies.append(pltpu.make_async_copy(ring.at[slot], grad.at[place], done.at[slot]))
        copies[-1].start()
    return copies[-slots:]


def weight_grad(layout, rows_cols, left, shares):
    spare = layout.spare
    count = len(shares)
    left_blocks, tokens, _ = left.shape
    hidden_blocks = shares[0].shape[0]

    def body(row_ref, col_ref, left_ref, *refs):
        share_refs, (grad, sum_ref, made, done, full, *wide) = refs[:count], refs[count:]
        gather_hidden(lax.axis_index("row"), share_refs, full)
        if spare:
            full[hidden_blocks] = jnp.zeros((tokens, BLK), BF16)
            wide[0][pl.ds(0, left_blocks)] = left_ref[...]
            wide[0][left_blocks] = jnp.zeros((tokens, BLK), BF16)
            left_ref = wide[0]
        copies = send_products(layout, row_ref, col_ref, left_ref, full, made, grad, done)
        for block in range(hidden_blocks):
            sum_ref[pl.ds(block, 1), :] = jnp.sum(full[block].astype(F32), axis=0, keepdims=True)
        for copy in copies:
            copy.wait()

    flops, moved = apply_cost(layout, tokens)
    out = shape_of((layout.capacity, BLK, BLK), F32)
    scratch = ring_scratch(layout)
    scratch += [pltpu.VMEM((hidden_blocks + spare, tokens, BLK), BF16)]
    if spare:
        scratch += [pltpu.VMEM((left_blocks + 1, tokens, BLK), BF16)]
    return call(
        body,
        [out, shape_of((hidden_blocks, BLK), F32)],
        [SM, SM, VM] + [VM] * count,
        [*rows_cols, left, *shares],
        scratch=scratch,
        out_specs=[pl.BlockSpec(memory_space=pltpu.HBM), VM],
        flops=flops,
        moved=2 * moved,
        limit=VMEM_GRAD,
    )


def add_up(own_ref, parts):
    total = own_ref[...]
    for part in parts:
        total = total + part[...].astype(F32)
    return total


def activate(own, parts, bias):
    def body(own_ref, bias_ref, *refs):
        parts, (value_ref, slope_ref) = refs[:-2], refs[-2:]
        hidden = add_up(own_ref, parts) + bias_ref[...][:, None, :]
        value, slope = gelu_parts(hidden)
        value_ref[...] = value.astype(BF16)
        slope_ref[...] = slope

    outs = [shape_of(own.shape, BF16), shape_of(own.shape, F32)]
    return call(body, outs, [VM] * (2 + len(parts)), [own, bias, *parts], moved=own.size * 20)


def scale_by_slope(own, parts, slope, after):
    def body(own_ref, slope_ref, after_ref, *refs):
        parts, (out_ref, token) = refs[:-2], refs[-2:]
        out_ref[...] = (add_up(own_ref, parts) * slope_ref[...]).astype(BF16)
        token[...] = jnp.zeros_like(token)

    outs = [shape_of(own.shape, BF16), shape_of((8, BLK), F32)]
    return call(body, outs, [VM] * (3 + len(parts)), [own, slope, after, *parts], moved=own.size * 16)


def pair_sums(*pairs):
    half, piece, width = pairs[0][0].shape
    count = len(pairs)

    def body(*refs):
        sources, owns, sends = refs[: 2 * count], refs[2 * count : 3 * count], refs[3 * count :]
        for which in range(count):
            keep, came = sources[2 * which : 2 * which + 2]
            owns[which][...] = keep[0] + came[0].astype(F32)
            for entry, send in enumerate(sends, 1):
                send[which] = (keep[entry] + came[entry].astype(F32)).astype(BF16)

    outs = [shape_of((piece, width), F32)] * count + [shape_of((count, piece, width), BF16)] * (half - 1)
    args = [array for pair in pairs for array in pair]
    results = call(body, outs, [VM] * len(args), args, moved=8 * count * half * piece * width)
    return results[:count], results[count:]


def final_sums(owns, parts):
    def body(*refs):
        sources, came, outs = refs[: len(owns)], refs[len(owns) : -len(owns)], refs[-len(owns) :]
        for which, (own, out) in enumerate(zip(sources, outs)):
            total = own[...]
            for part in came:
                total = total + part[which].astype(F32)
            out[...] = total.astype(BF16)

    outs = [shape_of(own.shape, BF16) for own in owns]
    return call(body, outs, [VM] * (len(owns) + len(parts)), [*owns, *parts], moved=8 * sum(own.size for own in owns))


def gather_col(shard, n_col, *before):
    shards = [None] * n_col
    shards[0] = shard
    for mask in range(2, n_col, 2):
        shards[mask] = swap(shard, "col", n_col, mask)
    for mask in range(2, n_col, 2):
        shards[mask] = follow(shards[mask], *before)
    for mask in range(0, n_col, 2):
        shards[mask + 1] = swap(shards[mask], "col", n_col, 1)
    return shards


def gather_row(share, n_row):
    return [share] + [swap(share, "row", n_row, mask) for mask in range(1, n_row)]


def send_row(sends, n_row):
    return [swap(send, "row", n_row, mask) for mask, send in enumerate(sends, 1)]


def local(n_row, n_col, tokens, cotangent, w1_mask, w1_blocks, bias, w2_mask, w2_blocks):
    first_blocks = w1_blocks[0, 0]
    second_blocks = w2_blocks[0, 0]
    model_blocks, hidden_blocks = w1_mask.shape
    first = Slots(w1_mask.shape, first_blocks.shape[0])
    second = Slots(w2_mask.shape, second_blocks.shape[0])
    first_at, second_at = slot_indices([first, second], [w1_mask, w2_mask])
    bias_wide = bias.astype(F32).reshape(hidden_blocks, BLK)

    first_held, first_there = fetch(first_blocks)
    second_held, second_there = fetch(second_blocks)
    shards = gather_col(together(tokens, cotangent), n_col, first_there, second_there)

    hidden_own, hidden_sends, full_tokens = model_to_hidden(
        first, first_at, shards, 0, first_held, True, hidden_blocks, n_row
    )
    hidden_parts = send_row(hidden_sends, n_row)
    act_own, act_sends, full_cotangent = model_to_hidden(
        second, second_at, shards, 1, second_held, False, hidden_blocks, n_row, after=(full_tokens,)
    )
    act_parts = send_row(act_sends, n_row)

    activated, slope = activate(hidden_own, hidden_parts, bias_wide)
    activated_shares = gather_row(activated, n_row)
    first_turned, turned_there = turn(first_held, slope)
    grad_hidden, grad_there = scale_by_slope(act_own, act_parts, slope, turned_there)
    met = swap(grad_there, "col", n_col, 1)
    grad_later = follow(grad_hidden, met)
    grad_shares = [grad_hidden]
    for mask in range(1, n_row):
        grad_shares += [swap(grad_hidden if mask == n_row - 1 else grad_later, "row", n_row, mask)]

    out_keep, out_send, out_done, w2_grad = hidden_to_model(
        second, second_at, activated_shares, second_held, True, model_blocks, n_col, other=full_cotangent
    )
    out_came = swap(out_send, "col", n_col, 1)
    in_keep, in_send = hidden_to_model(
        first, first_at, grad_shares, first_turned, False, model_blocks, n_col, after=(out_done,)
    )
    in_came = swap(in_send, "col", n_col, 1)
    owns, sends = pair_sums((out_keep, out_came), (in_keep, in_came))
    parts = [swap(send, "col", n_col, 2 * entry) for entry, send in enumerate(sends, 1)]
    w1_grad, bias_sum = weight_grad(first, first_at, full_tokens, grad_shares)
    out, tokens_grad = final_sums(owns, parts)
    return (
        out,
        tokens_grad,
        w1_grad[None, None],
        w2_grad[None, None],
        bias_sum.reshape(-1),
    )


def solution(mesh):
    n_row, n_col = mesh.shape["row"], mesh.shape["col"]
    return jax.shard_map(
        lambda *args: local(n_row, n_col, *args),
        mesh=mesh,
        in_specs=(
            P("col", "row"),
            P("col", "row"),
            P("row", "col"),
            P("row", "col", None, None, None),
            P("col"),
            P("col", "row"),
            P("row", "col", None, None, None),
        ),
        out_specs=(
            P("col", "row"),
            P("col", "row"),
            P("row", "col", None, None, None),
            P("row", "col", None, None, None),
            P("col"),
        ),
        check_vma=False,
    )
```

```python
import functools
import math

import jax
import jax.numpy as jnp
from jax import lax
from jax.experimental import pallas as pl
from jax.experimental.pallas import tpu as pltpu
from jax.sharding import PartitionSpec as P

BLK = 128
F32 = jnp.float32
BF16 = jnp.bfloat16
VMEM_LIMIT = 12 * 1024 * 1024
VMEM_GRAD = 28 * 1024 * 1024
RING = 24
GRAD_PARTS = (12, 16, 8, 6, 4, 3, 2, 1)

slope_const = math.sqrt(2.0 / math.pi)


def gelu_parts(values):
    inner = slope_const * (values + 0.044715 * values * values * values)
    tangent = jnp.tanh(inner)
    value = 0.5 * values * (1.0 + tangent)
    slope = 0.5 * (1.0 + tangent) + 0.5 * values * (1.0 - tangent * tangent) * slope_const * (
        1.0 + 3.0 * 0.044715 * values * values
    )
    return value, slope


def swap(array, axis, size, mask):
    return lax.ppermute(array, axis, [(place, place ^ mask) for place in range(size)])


def call(body, outs, in_specs, args, scratch=(), grid=None, out_specs=None, flops=0, moved=0, limit=VMEM_LIMIT):
    whole = pl.BlockSpec(memory_space=pltpu.VMEM)
    extra = {} if grid is None else {"grid": grid}
    return pl.pallas_call(
        body,
        out_shape=outs,
        in_specs=in_specs,
        out_specs=[whole] * len(outs) if out_specs is None else out_specs,
        scratch_shapes=list(scratch),
        compiler_params=pltpu.CompilerParams(vmem_limit_bytes=limit),
        cost_estimate=pl.CostEstimate(flops=flops, bytes_accessed=moved, transcendentals=0),
        **extra,
    )(*args)


VM = pl.BlockSpec(memory_space=pltpu.VMEM)
SM = pl.BlockSpec(memory_space=pltpu.SMEM)


def shape_of(shape, dtype):
    return jax.ShapeDtypeStruct(shape, dtype)


def dot(left, right, left_dim, right_dim):
    return lax.dot_general(
        left, right, (((left_dim,), (right_dim,)), ((), ())), preferred_element_type=F32
    )


class Slots:
    def __init__(self, mask_shape, capacity):
        self.rows, self.cols = mask_shape
        self.capacity = capacity
        self.even = self.cols % 8 == 0 and self.cols // 4 <= BLK and capacity == self.rows * (self.cols // 4)
        self.group = self.cols // 4 if self.even else 1
        self.groups = capacity // self.group
        self.spare = 0 if self.even else 1

    def uneven_slots(self, mask):
        self.even, self.group, self.groups, self.spare = False, 1, self.capacity, 1
        flat = mask.reshape(-1)
        count = flat.shape[0]
        places = jnp.arange(count, dtype=jnp.int32)
        lane = jnp.arange(self.cols, dtype=jnp.int32)
        within = jnp.sum(jnp.where(lane[None, :] <= lane[:, None], mask[:, None, :], 0), axis=2)
        row_sum = jnp.sum(mask, axis=1)
        line = jnp.arange(self.rows, dtype=jnp.int32)
        before = jnp.sum(jnp.where(line[None, :] < line[:, None], row_sum[None, :], 0), axis=1)
        rank = (within + before[:, None] - 1).reshape(-1)
        slot = jnp.arange(self.capacity, dtype=jnp.int32)
        hit = (rank[None, :] == slot[:, None]) & (flat[None, :] > 0)
        order = jnp.sum(jnp.where(hit, places[None, :], 0), axis=1)
        live = slot < jnp.sum(flat)
        row = jnp.where(live, order // self.cols, self.rows)
        col = jnp.where(live, order % self.cols, self.cols)
        return row, col


def index_kernel(layout, mask, out_ref):
    rows, cols, group = layout.rows, layout.cols, layout.group
    lower = lax.broadcasted_iota(jnp.int32, (cols, cols), 0)
    upper = lax.broadcasted_iota(jnp.int32, (cols, cols), 1)
    ramp = jnp.where(lower <= upper, 1.0, 0.0).astype(BF16)
    rank = dot(mask.astype(BF16), ramp, 1, 0)
    place = lax.broadcasted_iota(jnp.int32, (rows, cols), 1).astype(F32)
    lane = lax.broadcasted_iota(jnp.int32, (rows, BLK), 1)
    found = jnp.zeros((rows, BLK), F32)
    for slot in range(group):
        hit = (rank == float(slot + 1)) & (mask > 0.0)
        column = jnp.sum(jnp.where(hit, place, 0.0), axis=1, keepdims=True)
        found = jnp.where(lane == slot, column, found)
    out_ref[...] = found.astype(jnp.int32)


def slot_indices(layouts, masks):
    if not all(layout.even for layout in layouts):
        return [layout.uneven_slots(mask) for layout, mask in zip(layouts, masks)]
    turned = [layout.rows > layout.cols for layout in layouts]
    arrays = [mask.T if turn else mask for mask, turn in zip(masks, turned)]

    def body(*refs):
        for which, (layout, turn) in enumerate(zip(layouts, turned)):
            mask = refs[which][...].astype(F32)
            index_kernel(layout, mask.T if turn else mask, refs[len(layouts) + which])

    outs = call(
        body,
        [shape_of((layout.rows, BLK), jnp.int32) for layout in layouts],
        [pl.BlockSpec(array.shape, lambda step: (0, 0)) for array in arrays],
        [pltpu.with_memory_space_constraint(array, pltpu.HBM) for array in arrays],
        grid=(1,),
    )
    return [(out, out) for out in outs]


def read_slot(layout, row_ref, col_ref, group, member):
    if layout.even:
        return group, col_ref[group, member]
    return row_ref[group], col_ref[group]


def add_forward(layout, row_ref, col_ref, first, here, source, blocks, total):
    group = layout.group
    for near in range(here):
        if layout.even:
            left = source[first + near]
            width = 2 if group % 2 == 0 else 1
            for member in range(0, group, width):
                place = near * group + member
                right = [blocks[place + more] for more in range(width)]
                right = right[0] if width == 1 else jnp.concatenate(right, axis=1)
                product = dot(left, right, 1, 0)
                for more in range(width):
                    col = col_ref[first + near, member + more]
                    total[col] += product[:, more * BLK : (more + 1) * BLK]
        else:
            row, col = read_slot(layout, row_ref, col_ref, first + near, 0)
            total[col] += dot(source[row], blocks[near], 1, 0)


def add_backward(layout, row_ref, col_ref, first, here, source, blocks, total, turned=False):
    group = layout.group
    side = 0 if turned else 1
    for near in range(here):
        if layout.even:
            width = 2 if group % 2 == 0 else 1
            result = None
            for member in range(0, group, width):
                place = near * group + member
                cols = [col_ref[first + near, member + more] for more in range(width)]
                left = [source[col] for col in cols]
                right = [blocks[place + more] for more in range(width)]
                left = left[0] if width == 1 else jnp.concatenate(left, axis=1)
                right = right[0] if width == 1 else jnp.concatenate(right, axis=side)
                product = dot(left, right, 1, side)
                result = product if result is None else result + product
            total[first + near] = result
        else:
            row, col = read_slot(layout, row_ref, col_ref, first + near, 0)
            total[row] += dot(source[col], blocks[near], 1, side)


def block_products(layout, row_ref, col_ref, first, here, left, right, out):
    group = layout.group
    for near in range(here):
        if layout.even:
            turned = left[first + near].T
            width = 2 if group % 2 == 0 else 1
            for member in range(0, group, width):
                place = near * group + member
                cols = [col_ref[first + near, member + more] for more in range(width)]
                wide = [right[col] for col in cols]
                wide = wide[0] if width == 1 else jnp.concatenate(wide, axis=1)
                product = dot(turned, wide, 1, 0)
                for more in range(width):
                    out[place + more] = product[:, more * BLK : (more + 1) * BLK]
        else:
            row, col = read_slot(layout, row_ref, col_ref, first + near, 0)
            live = row < layout.rows
            product = dot(left[row].T, right[col], 1, 0)
            out[near] = jnp.where(live, product, 0.0)


def gather_model(me, shards, which, stage, full):
    piece = shards[0].shape[1]
    for mask, shard in enumerate(shards):
        start = pl.multiple_of((me ^ mask) * piece, piece)
        stage[pl.ds(start, piece), :] = shard[which].astype(F32)
    for block in range(shards[0].shape[2] // BLK):
        full[block] = stage[:, block * BLK : (block + 1) * BLK].astype(full.dtype)


def gather_hidden(me, shares, full):
    blocks, piece, _ = shares[0].shape
    for mask, share in enumerate(shares):
        start = pl.multiple_of((me ^ mask) * piece, piece)
        full[pl.ds(0, blocks), pl.ds(start, piece), :] = share[...]


def parts_of(layout, choices):
    parts = next(parts for parts in choices if layout.groups % parts == 0)
    return parts, layout.groups // parts, layout.capacity // parts


def apply_cost(layout, tokens):
    return 2 * layout.capacity * BLK * BLK * tokens, 2 * layout.capacity * BLK * BLK


def together(first, second):
    def body(first_ref, second_ref, out_ref):
        out_ref[0] = first_ref[...]
        out_ref[1] = second_ref[...]

    block = pl.BlockSpec(first.shape, lambda step: (0, 0))
    return call(
        body,
        [shape_of((2, *first.shape), first.dtype)],
        [block, block],
        [pltpu.with_memory_space_constraint(array, pltpu.HBM) for array in (first, second)],
        grid=(1,),
        moved=8 * first.size,
    )[0]


def fetch(blocks):
    def body(from_ref, to_ref, token, done):
        copy = pltpu.make_async_copy(from_ref, to_ref, done)
        copy.start()
        token[...] = jnp.zeros_like(token)
        copy.wait()

    return call(
        body,
        [pltpu.VMEM(blocks.shape, blocks.dtype), shape_of((8, BLK), F32)],
        [pl.BlockSpec(memory_space=pltpu.HBM)],
        [pltpu.with_memory_space_constraint(blocks, pltpu.HBM)],
        scratch=[pltpu.SemaphoreType.DMA],
        moved=4 * blocks.size,
    )


def follow(array, *before):
    def body(array_ref, *refs):
        refs[-1][...] = array_ref[...]

    specs = [VM] * (1 + len(before))
    return call(body, [shape_of(array.shape, array.dtype)], specs, [array, *before], moved=4 * array.size)[0]


def turn(blocks, after):
    count = blocks.shape[0]

    def body(from_ref, after_ref, to_ref, token):
        token[...] = jnp.zeros_like(token)

        def one(place, carry):
            to_ref[place] = from_ref[place].T
            return carry

        lax.fori_loop(0, count, one, 0, unroll=math.gcd(count, 48))

    return call(
        body,
        [pltpu.VMEM(blocks.shape, blocks.dtype), shape_of((8, BLK), F32)],
        [VM, VM],
        [pltpu.with_memory_space_constraint(blocks, pltpu.VMEM), after],
        moved=2 * blocks.size,
    )


def model_to_hidden(layout, rows_cols, shards, which, blocks, forward, hidden_blocks, n_row, after=()):
    count = len(shards)
    _, part, width = shards[0].shape
    tokens = part * count
    model_blocks = width // BLK
    piece = tokens // n_row
    spare = layout.spare

    def body(row_ref, col_ref, *refs):
        shard_refs = refs[:count]
        weights, own, *sends, full, stage, total = refs[count + len(after) :]
        gather_model(lax.axis_index("col"), shard_refs, which, stage, full)
        if spare:
            full[model_blocks] = jnp.zeros((tokens, BLK), BF16)
        if forward or spare:
            total[...] = jnp.zeros_like(total)
        work = add_forward if forward else add_backward
        work(layout, row_ref, col_ref, 0, layout.groups, full, weights, total)
        me = lax.axis_index("row")
        for mask, out in enumerate([own] + sends):
            start = pl.multiple_of((me ^ mask) * piece, piece)
            out[...] = total[pl.ds(0, hidden_blocks), pl.ds(start, piece), :].astype(out.dtype)

    share = (hidden_blocks, piece, BLK)
    outs = [shape_of(share, F32)] + [shape_of(share, BF16)] * (n_row - 1)
    outs += [shape_of((model_blocks + spare, tokens, BLK), BF16)]
    flops, moved = apply_cost(layout, tokens)
    args = [*rows_cols, *shards, *after, pltpu.with_memory_space_constraint(blocks, pltpu.VMEM)]
    own, *sends, whole = call(
        body,
        outs,
        [SM, SM] + [VM] * (len(args) - 2),
        args,
        scratch=[
            pltpu.VMEM((tokens, width), F32),
            pltpu.VMEM((hidden_blocks + spare, tokens, BLK), F32),
        ],
        flops=flops,
        moved=moved,
    )
    return own, sends, whole


def hidden_to_model(layout, rows_cols, shares, blocks, forward, model_blocks, n_col, other=None, after=()):
    count = len(shares)
    hidden_blocks, part, _ = shares[0].shape
    tokens = part * count
    piece = tokens // n_col
    half = n_col // 2
    spare = layout.spare
    grads = other is not None

    def body(row_ref, col_ref, *refs):
        share_refs, refs = refs[:count], refs[count + len(after) :]
        if grads:
            other_ref, weights, keep, send, token, grad, full, total, made, done = refs
            token[...] = jnp.zeros_like(token)
        else:
            weights, keep, send, full, total = refs
        gather_hidden(lax.axis_index("row"), share_refs, full)
        if spare:
            full[hidden_blocks] = jnp.zeros((tokens, BLK), BF16)
        if forward or spare:
            total[...] = jnp.zeros_like(total)
        if grads:
            copies = send_products(layout, row_ref, col_ref, full, other_ref, made, grad, done)
        work = add_forward if forward else functools.partial(add_backward, turned=True)
        work(layout, row_ref, col_ref, 0, layout.groups, full, weights, total)
        me = lax.axis_index("col")
        for entry in range(half):
            mine = pl.multiple_of((me ^ (2 * entry)) * piece, piece)
            theirs = pl.multiple_of((me ^ (2 * entry + 1)) * piece, piece)
            for block in range(model_blocks):
                lanes = pl.ds(block * BLK, BLK)
                keep[entry, :, lanes] = total[block, pl.ds(mine, piece), :]
                send[entry, :, lanes] = total[block, pl.ds(theirs, piece), :].astype(BF16)
        if grads:
            for copy in copies:
                copy.wait()

    pair = (half, piece, model_blocks * BLK)
    outs = [shape_of(pair, F32), shape_of(pair, BF16)]
    whole = shape_of((hidden_blocks + spare, tokens, BLK), BF16)
    out_specs = [VM] * (4 if grads else 3)
    args = [*rows_cols, *shares, *after]
    scratch = [pltpu.VMEM((model_blocks + spare, tokens, BLK), F32)]
    flops, moved = apply_cost(layout, tokens)
    if grads:
        outs += [shape_of((8, BLK), F32), shape_of((layout.capacity, BLK, BLK), F32)]
        out_specs[3] = pl.BlockSpec(memory_space=pltpu.HBM)
        args += [other]
        scratch = [pltpu.VMEM(whole.shape, BF16), *scratch, *ring_scratch(layout)]
        flops, moved = 2 * flops, 3 * moved
    else:
        outs += [whole]
    args += [pltpu.with_memory_space_constraint(blocks, pltpu.VMEM)]
    return call(
        body,
        outs,
        [SM, SM] + [VM] * (len(args) - 2),
        args,
        scratch=scratch,
        out_specs=out_specs,
        flops=flops,
        moved=moved,
        limit=VMEM_GRAD if grads else VMEM_LIMIT,
    )


def ring_scratch(layout):
    parts, _, size = parts_of(layout, GRAD_PARTS)
    slots = min(RING, parts)
    return [pltpu.VMEM((slots, size, BLK, BLK), F32), pltpu.SemaphoreType.DMA((slots,))]


def send_products(layout, row_ref, col_ref, left, right, ring, grad, done):
    parts, here, size = parts_of(layout, GRAD_PARTS)
    slots = ring.shape[0]
    copies = []
    for part in range(parts):
        slot = part % slots
        if part >= slots:
            copies[part - slots].wait()
        block_products(layout, row_ref, col_ref, part * here, here, left, right, ring.at[slot])
        place = pl.ds(part * size, size)
        copies.append(pltpu.make_async_copy(ring.at[slot], grad.at[place], done.at[slot]))
        copies[-1].start()
    return copies[-slots:]


def weight_grad(layout, rows_cols, left, right, hidden_blocks):
    def body(row_ref, col_ref, left_ref, right_ref, grad, sum_ref, made, done):
        copies = send_products(layout, row_ref, col_ref, left_ref, right_ref, made, grad, done)
        for block in range(hidden_blocks):
            sum_ref[pl.ds(block, 1), :] = jnp.sum(right_ref[block].astype(F32), axis=0, keepdims=True)
        for copy in copies:
            copy.wait()

    flops, moved = apply_cost(layout, left.shape[1])
    return call(
        body,
        [shape_of((layout.capacity, BLK, BLK), F32), shape_of((hidden_blocks, BLK), F32)],
        [SM, SM, VM, VM],
        [*rows_cols, left, right],
        scratch=ring_scratch(layout),
        out_specs=[pl.BlockSpec(memory_space=pltpu.HBM), VM],
        flops=flops,
        moved=2 * moved,
        limit=VMEM_GRAD,
    )


def add_up(own_ref, parts):
    total = own_ref[...]
    for part in parts:
        total = total + part[...].astype(F32)
    return total


def activate(own, parts, bias):
    def body(own_ref, bias_ref, *refs):
        parts, (value_ref, slope_ref) = refs[:-2], refs[-2:]
        hidden = add_up(own_ref, parts) + bias_ref[...][:, None, :]
        value, slope = gelu_parts(hidden)
        value_ref[...] = value.astype(BF16)
        slope_ref[...] = slope

    outs = [shape_of(own.shape, BF16), shape_of(own.shape, F32)]
    return call(body, outs, [VM] * (2 + len(parts)), [own, bias, *parts], moved=own.size * 20)


def scale_by_slope(own, parts, slope, after):
    def body(own_ref, slope_ref, after_ref, *refs):
        parts, (out_ref, token) = refs[:-2], refs[-2:]
        out_ref[...] = (add_up(own_ref, parts) * slope_ref[...]).astype(BF16)
        token[...] = jnp.zeros_like(token)

    outs = [shape_of(own.shape, BF16), shape_of((8, BLK), F32)]
    return call(body, outs, [VM] * (3 + len(parts)), [own, slope, after, *parts], moved=own.size * 16)


def pair_sums(*pairs):
    half, piece, width = pairs[0][0].shape
    count = len(pairs)

    def body(*refs):
        sources, owns, sends = refs[: 2 * count], refs[2 * count : 3 * count], refs[3 * count :]
        for which in range(count):
            keep, came = sources[2 * which : 2 * which + 2]
            owns[which][...] = keep[0] + came[0].astype(F32)
            for entry, send in enumerate(sends, 1):
                send[which] = (keep[entry] + came[entry].astype(F32)).astype(BF16)

    outs = [shape_of((piece, width), F32)] * count + [shape_of((count, piece, width), BF16)] * (half - 1)
    args = [array for pair in pairs for array in pair]
    results = call(body, outs, [VM] * len(args), args, moved=8 * count * half * piece * width)
    return results[:count], results[count:]


def final_sums(owns, parts):
    def body(*refs):
        sources, came, outs = refs[: len(owns)], refs[len(owns) : -len(owns)], refs[-len(owns) :]
        for which, (own, out) in enumerate(zip(sources, outs)):
            total = own[...]
            for part in came:
                total = total + part[which].astype(F32)
            out[...] = total.astype(BF16)

    outs = [shape_of(own.shape, BF16) for own in owns]
    return call(body, outs, [VM] * (len(owns) + len(parts)), [*owns, *parts], moved=8 * sum(own.size for own in owns))


def gather_col(shard, n_col, *before):
    shards = [None] * n_col
    shards[0] = shard
    for mask in range(2, n_col, 2):
        shards[mask] = swap(shard, "col", n_col, mask)
    for mask in range(2, n_col, 2):
        shards[mask] = follow(shards[mask], *before)
    for mask in range(0, n_col, 2):
        shards[mask + 1] = swap(shards[mask], "col", n_col, 1)
    return shards


def gather_row(share, n_row):
    return [share] + [swap(share, "row", n_row, mask) for mask in range(1, n_row)]


def send_row(sends, n_row):
    return [swap(send, "row", n_row, mask) for mask, send in enumerate(sends, 1)]


def local(n_row, n_col, tokens, cotangent, w1_mask, w1_blocks, bias, w2_mask, w2_blocks):
    first_blocks = w1_blocks[0, 0]
    second_blocks = w2_blocks[0, 0]
    model_blocks, hidden_blocks = w1_mask.shape
    first = Slots(w1_mask.shape, first_blocks.shape[0])
    second = Slots(w2_mask.shape, second_blocks.shape[0])
    first_at, second_at = slot_indices([first, second], [w1_mask, w2_mask])
    bias_wide = bias.astype(F32).reshape(hidden_blocks, BLK)

    first_held, first_there = fetch(first_blocks)
    second_held, second_there = fetch(second_blocks)
    shards = gather_col(together(tokens, cotangent), n_col, first_there, second_there)

    hidden_own, hidden_sends, full_tokens = model_to_hidden(
        first, first_at, shards, 0, first_held, True, hidden_blocks, n_row
    )
    hidden_parts = send_row(hidden_sends, n_row)
    act_own, act_sends, full_cotangent = model_to_hidden(
        second, second_at, shards, 1, second_held, False, hidden_blocks, n_row, after=(full_tokens,)
    )
    act_parts = send_row(act_sends, n_row)

    activated, slope = activate(hidden_own, hidden_parts, bias_wide)
    activated_shares = gather_row(activated, n_row)
    first_turned, turned_there = turn(first_held, slope)
    grad_hidden, grad_there = scale_by_slope(act_own, act_parts, slope, turned_there)
    met = swap(grad_there, "col", n_col, 1)
    grad_later = follow(grad_hidden, met)
    grad_shares = [grad_hidden]
    for mask in range(1, n_row):
        grad_shares += [swap(grad_hidden if mask == n_row - 1 else grad_later, "row", n_row, mask)]

    out_keep, out_send, out_done, w2_grad = hidden_to_model(
        second, second_at, activated_shares, second_held, True, model_blocks, n_col, other=full_cotangent
    )
    out_came = swap(out_send, "col", n_col, 1)
    in_keep, in_send, full_grad = hidden_to_model(
        first, first_at, grad_shares, first_turned, False, model_blocks, n_col, after=(out_done,)
    )
    in_came = swap(in_send, "col", n_col, 1)
    owns, sends = pair_sums((out_keep, out_came), (in_keep, in_came))
    parts = [swap(send, "col", n_col, 2 * entry) for entry, send in sorted(enumerate(sends, 1), key=lambda e: e[0] == 1)]
    w1_grad, bias_sum = weight_grad(first, first_at, full_tokens, full_grad, hidden_blocks)
    out, tokens_grad = final_sums(owns, parts)
    return (
        out,
        tokens_grad,
        w1_grad[None, None],
        w2_grad[None, None],
        bias_sum.reshape(-1),
    )


def solution(mesh):
    n_row, n_col = mesh.shape["row"], mesh.shape["col"]
    return jax.shard_map(
        lambda *args: local(n_row, n_col, *args),
        mesh=mesh,
        in_specs=(
            P("col", "row"),
            P("col", "row"),
            P("row", "col"),
            P("row", "col", None, None, None),
            P("col"),
            P("col", "row"),
            P("row", "col", None, None, None),
        ),
        out_specs=(
            P("col", "row"),
            P("col", "row"),
            P("row", "col", None, None, None),
            P("row", "col", None, None, None),
            P("col"),
        ),
        check_vma=False,
    )
```
